256 devices in a mesh: fsdp: 16 (over z, core), tensor: 16 (over y, x).
Axes of the slice: x: 4, y: 4, z: 8, core: 2. Of those that a mesh axis runs over, the one named last changes fastest.
Arguments:
- momentum: float32 [8192, 14336], P('fsdp', 'tensor'), may hold values from -1000 to 1000
- gradient: bfloat16 [8192, 14336], P('fsdp', 'tensor'), may hold values from -6 to 6
- right_state: float32 [14336, 256], P('tensor'), may hold values from -6 to 6
Outputs:
- momentum_next: float32 [8192, 14336], P('fsdp', 'tensor')
- right_next: float32 [14336, 256], P('tensor')
- step_direction: float32 [8192, 14336], P('fsdp', 'tensor')
The draws below stay inside these ranges and needn't reach their ends.
All inputs are finite; a program needn't handle non-finite values.
Results may differ from the reference program's by a relative error of at most 0.0003.
Values sent between devices are 32-bit elements; how exact they have to be, the bound alone decides.
No kernel may reach another device: no remote copies, remote signals or barrier semaphores. Data moves between devices by JAX's collectives and lax.ppermute only.
A program may use at most 64 MiB of HBM per device.

```python
import math
import jax
import jax.numpy as jnp
from jax import lax

D = 8192
FFW = 14336
RANK = 256


def draw_momentum(key, part):
    key = jax.random.fold_in(key, 7)
    keys_list = jax.random.split(key, 6)
    row_place = jnp.arange(D, dtype=jnp.float32) / max(D - 1, 1)
    column_place = jnp.arange(FFW, dtype=jnp.float32) / max(FFW - 1, 1)
    values_base = jax.random.truncated_normal(keys_list[0], -6.0, 6.0, (D, FFW), jnp.float32)
    spread_log = math.log(10.0)
    trend_log = math.log(3.0)
    outer_size = 60.0
    row_scale = jnp.exp(spread_log * (jax.random.uniform(keys_list[1], (D, 1), jnp.float32) - 0.5) + trend_log * (row_place[:, None] - 0.5))
    column_scale = jnp.exp(spread_log * (jax.random.uniform(keys_list[2], (1, FFW), jnp.float32) - 0.5) + trend_log * (column_place[None, :] - 0.5))
    row_vector = jax.random.uniform(keys_list[4], (D, 1), jnp.float32, -1.7320508, 1.7320508)
    column_vector = jax.random.uniform(keys_list[5], (1, FFW), jnp.float32, -1.7320508, 1.7320508)
    values_all = values_base * row_scale * column_scale + outer_size * row_vector * column_vector
    return jnp.clip(values_all, -1000.0, 1000.0)


def draw_right_state(key, part):
    key = jax.random.fold_in(key, 11)
    keys_list = jax.random.split(key, 2)
    values_base = jax.random.truncated_normal(keys_list[0], -6.0, 6.0, (FFW, RANK), jnp.float32)
    spread_log = math.log(1000.0)
    column_order = jax.random.permutation(keys_list[1], RANK).astype(jnp.float32) / max(RANK - 1, 1)
    column_scale = jnp.exp(-spread_log * column_order)
    return values_base * column_scale[None, :]


def shard_levels(key, extent, cuts, least, high):
    level, own = 1.0, jax.random.fold_in(key, 6)
    for dim, blocks in cuts:
        draws = jnp.exp(jax.random.uniform(jax.random.fold_in(own, dim), (blocks,), jnp.float32, least / len(cuts), high / len(cuts)))
        level = level * jnp.repeat(draws, extent[dim] // blocks).reshape([-1 if axis == dim else 1 for axis in range(len(extent))])
    return level


def centred(stream_key, dims, deviation, reach, shards=(), held_as=jnp.bfloat16):
    array = deviation * jax.random.normal(stream_key, dims, jnp.float32)
    if shards:
        array = array * shard_levels(stream_key, dims, shards, -0.22, 0.18)
    return jnp.clip(array, -reach, reach).astype(held_as)


def setup_inputs(seed: int = 0) -> dict:
    keys = jax.random.split(jax.random.key(seed), 4)
    return {
        "momentum": draw_momentum(jax.random.fold_in(keys[3], 71), 0),
        "gradient": centred(keys[1], (D, FFW), 1.0, 6.0, ((0, 16), (1, 16))),
        "right_state": draw_right_state(jax.random.fold_in(keys[3], 71), 0),
    }


highest = lax.Precision.HIGHEST
error_share = 0.05

def matmul_cols(left_side, right_side):
    return lax.dot_general(left_side.astype(jnp.float32), right_side.astype(jnp.float32), (((1,), (1,)), ((), ())), precision=highest, preferred_element_type=jnp.float32)

def matmul_rows(left_side, right_side):
    return lax.dot_general(left_side.astype(jnp.float32), right_side.astype(jnp.float32), (((0,), (0,)), ((), ())), precision=highest, preferred_element_type=jnp.float32)

def inverse_factor(gram_matrix):
    identity = jnp.eye(RANK, dtype=gram_matrix.dtype)
    ridge_term = 1e-06 * jnp.trace(gram_matrix) / RANK
    cholesky_factor = jnp.linalg.cholesky(gram_matrix + ridge_term * identity)
    return jax.scipy.linalg.solve_triangular(cholesky_factor, identity, lower=True)

def reference(momentum, gradient, right_state):
    buffer = momentum + gradient.astype(jnp.float32)
    left_basis = jnp.dot(buffer.astype(jnp.float32), right_state.astype(jnp.float32), precision=highest, preferred_element_type=jnp.float32)
    for sweep_index in range(2):
        gram_matrix = matmul_rows(left_basis, left_basis)
        left_basis = matmul_cols(left_basis, inverse_factor(gram_matrix))
    right_factor = matmul_rows(buffer, left_basis)
    mean_square = lax.optimization_barrier(jnp.sum(right_factor * right_factor, axis=0)) / FFW
    right_next = right_factor * lax.rsqrt(mean_square + 1e-06)
    momentum_next = buffer - error_share * matmul_cols(left_basis, right_factor)
    step_direction = math.sqrt(D / RANK) * matmul_cols(left_basis, right_next)
    return (momentum_next, right_next, step_direction)
```

```python
import math

import jax
import jax.numpy as jnp
from jax import lax
from jax.experimental import pallas as pl
from jax.experimental.pallas import tpu as pltpu
from jax.sharding import PartitionSpec as P

D = 8192
FFW = 14336
RANK = 256
BLOCK = 64
TENSOR = 16
Z = 8

highest = lax.Precision.HIGHEST
error_share = 0.05
z_groups = [[2 * z + core for z in range(Z)] for core in range(2)]


def multiply(left_side, right_side, left_dim, right_dim, precision=highest):
    return lax.dot_general(
        left_side,
        right_side,
        (((left_dim,), (right_dim,)), ((), ())),
        precision=precision,
        preferred_element_type=jnp.float32,
    )


def spread_lane(tile, lane):
    return jnp.broadcast_to(tile[:, lane : lane + 1], tile.shape)


def spread_row(tile, row):
    return jnp.broadcast_to(tile[row : row + 1, :], tile.shape)


def factor_block(tiles, first_lane, row_index):
    tiles = list(tiles)
    count = len(tiles)
    for s in range(count):
        columns = [
            {i: spread_lane(tiles[i], first_lane + 8 * s + j) for i in range(s, count)}
            for j in range(8)
        ]
        multipliers = []
        for k in range(8):
            inverse_pivot = 1.0 / spread_row(columns[k][s], k)
            multiplier = {i: columns[k][i] * inverse_pivot for i in range(s, count)}
            multiplier[s] = jnp.where(row_index > k, multiplier[s], 0.0)
            multipliers.append(multiplier)
            for j in range(k + 1, 8):
                pivot_row = spread_row(columns[j][s], k)
                for i in range(s, count):
                    columns[j][i] = columns[j][i] - multiplier[i] * pivot_row
        pivots = columns[0][s]
        for k in range(1, 8):
            pivots = jnp.where(row_index == k, columns[k][s], pivots)
        own = tiles[s]
        for k in range(8):
            pivot_row = spread_row(own, k)
            own = own - multipliers[k][s] * pivot_row
            for i in range(s + 1, count):
                tiles[i] = tiles[i] - multipliers[k][i] * pivot_row
        tiles[s] = own * lax.rsqrt(pivots)
    return tiles


def inverse_kernel(gram_ref, inverse_ref, work_ref):
    gram = gram_ref[...]
    rows = lax.broadcasted_iota(jnp.int32, (RANK, RANK), 0)
    lanes = lax.broadcasted_iota(jnp.int32, (RANK, RANK), 1)
    diagonal = rows == lanes
    ridge = (1e-06 / RANK) * jnp.sum(jnp.where(diagonal, gram, 0.0), keepdims=True)
    work_ref[:, :RANK] = gram + jnp.where(diagonal, ridge, 0.0)
    work_ref[:, RANK:] = jnp.where(diagonal, 1.0, 0.0)
    row_index = lax.broadcasted_iota(jnp.int32, (8, 128), 0)
    lane_index = lax.broadcasted_iota(jnp.int32, (8, 128), 1)
    for block in range(RANK // BLOCK):
        top = block * BLOCK
        aligned = top // 128 * 128
        first_lane = top - aligned
        own_half = lane_index >= 64 if first_lane else lane_index < 64
        tiles = []
        for i in range(BLOCK // 8):
            part = work_ref[top + 8 * i : top + 8 * i + 8, aligned : aligned + 128]
            unit = jnp.where(lane_index == row_index + (8 * i + 64 - first_lane), 1.0, 0.0)
            tiles.append(jnp.where(own_half, part, unit))
        factored = jnp.concatenate(factor_block(tiles, first_lane, row_index), axis=0)
        if first_lane == 0:
            factored = pltpu.roll(factored, 64, 1)
        done = multiply(factored[:, :BLOCK], work_ref[top : top + BLOCK, :], 1, 0)
        inverse_ref[top : top + BLOCK, :] = done[:, RANK:]
        if top + BLOCK < RANK:
            below = top + BLOCK
            start = below // 128 * 128
            update = multiply(done[:, start:RANK], done, 0, 0)
            work_ref[below:, :] = work_ref[below:, :] - update[below - start :, :]


def inverse_factor(gram_matrix):
    return pl.pallas_call(
        inverse_kernel,
        out_shape=jax.ShapeDtypeStruct((RANK, RANK), jnp.float32),
        in_specs=[pl.BlockSpec(memory_space=pltpu.VMEM)],
        out_specs=pl.BlockSpec(memory_space=pltpu.VMEM),
        scratch_shapes=[pltpu.VMEM((RANK, 2 * RANK), jnp.float32)],
        compiler_params=pltpu.CompilerParams(vmem_limit_bytes=16 * 1024 * 1024),
        name="inverse_factor",
    )(gram_matrix)


def exchange(block, axis, groups=None):
    return lax.all_to_all(block, axis, 0, 0, axis_index_groups=groups, tiled=True)


def share(block, axis, members, groups=None):
    whole = exchange(jnp.broadcast_to(block, (members,) + block.shape), axis, groups)
    return whole


def swap_cores(block):
    return lax.ppermute(block, "fsdp", [(i, i ^ 1) for i in range(2 * Z)])


def core_half(block, core):
    half = block.shape[0] // 2
    kept = lax.dynamic_slice_in_dim(block, core * half, half)
    given = lax.dynamic_slice_in_dim(block, (1 - core) * half, half)
    return kept + swap_cores(given)


def both_halves(half, core):
    other = swap_cores(half)
    first = jnp.where(core == 0, half, other)
    second = jnp.where(core == 0, other, half)
    return jnp.concatenate([first, second], axis=0)


def per_device(momentum, gradient, right_state):
    core = lax.axis_index("fsdp") % 2
    buffer = momentum + gradient.astype(jnp.float32)
    partial_left = multiply(buffer, right_state, 1, 0)
    rows = partial_left.shape[0]
    own_rows = jnp.sum(
        exchange(partial_left.reshape(TENSOR, rows // TENSOR, RANK), "tensor"), axis=0
    )
    left_raw = share(own_rows, "tensor", TENSOR).reshape(rows, RANK)

    gram_half = core_half(multiply(left_raw, left_raw, 0, 0), core)
    gram_half = jnp.sum(share(gram_half, "fsdp", Z, z_groups), axis=0)
    left_once = multiply(left_raw, inverse_factor(both_halves(gram_half, core)), 1, 1)

    columns = buffer.shape[1]
    products = jnp.concatenate(
        [multiply(buffer, left_once, 0, 0), multiply(left_once, left_once, 0, 0)], axis=0
    )
    half = core_half(products, core)
    piece = jnp.sum(
        exchange(half.reshape(Z, half.shape[0] // Z, RANK), "fsdp", z_groups), axis=0
    )
    half = share(piece, "fsdp", Z, z_groups).reshape(half.shape)
    products = both_halves(half, core)

    inverse = inverse_factor(products[columns:])
    left_basis = multiply(left_once, inverse, 1, 1)
    right_factor = multiply(products[:columns], inverse, 1, 1)
    square_sum = jnp.sum(right_factor * right_factor, axis=0)
    square_sum = jnp.sum(share(square_sum[None], "tensor", TENSOR), axis=(0, 1))
    mean_square = square_sum / FFW
    right_next = right_factor * lax.rsqrt(mean_square + 1e-06)
    momentum_next = buffer - error_share * multiply(left_basis, right_factor, 1, 1)
    step_direction = math.sqrt(D / RANK) * multiply(left_basis, right_next, 1, 1)
    return (momentum_next, right_next, step_direction)


def solution(mesh):
    return jax.shard_map(
        per_device,
        mesh=mesh,
        in_specs=(P("fsdp", "tensor"), P("fsdp", "tensor"), P("tensor", None)),
        out_specs=(P("fsdp", "tensor"), P("tensor", None), P("fsdp", "tensor")),
        check_vma=False,
    )
```

```python
import math

import jax
import jax.numpy as jnp
from jax import lax
from jax.experimental import pallas as pl
from jax.experimental.pallas import tpu as pltpu
from jax.sharding import PartitionSpec as P

D = 8192
FFW = 14336
RANK = 256
BLOCK = 64
HALF = RANK // 2
VMEM = 20 * 2**20
TENSOR = 16
Z = 8

highest = lax.Precision.HIGHEST
error_share = 0.05
z_groups = [[2 * z + core for z in range(Z)] for core in range(2)]


def multiply(left_side, right_side, left_dim, right_dim, precision=highest):
    return lax.dot_general(
        left_side,
        right_side,
        (((left_dim,), (right_dim,)), ((), ())),
        precision=precision,
        preferred_element_type=jnp.float32,
    )


def spread_lane(tile, lane):
    return jnp.take_along_axis(tile, jnp.full(tile.shape, lane, jnp.int32), axis=1)


def spread_row(tile, row):
    return jnp.broadcast_to(tile[row : row + 1, :], tile.shape)


def factor_block(tiles, first_lane, row_index):
    tiles = list(tiles)
    count = len(tiles)
    for s in range(count):
        columns = [
            {i: spread_lane(tiles[i], first_lane + 8 * s + j) for i in range(s, count)}
            for j in range(8)
        ]
        multipliers = []
        for k in range(8):
            inverse_pivot = 1.0 / spread_row(columns[k][s], k)
            multiplier = {i: columns[k][i] * inverse_pivot for i in range(s, count)}
            below = jnp.where(row_index > k, multiplier[s], 0.0)
            multipliers.append({**multiplier, s: below})
            for j in range(k + 1, 8):
                pivot_row = spread_row(columns[j][s], k)
                for i in range(s, count):
                    columns[j][i] = columns[j][i] - multiplier[i] * pivot_row
        pivots = columns[0][s]
        for k in range(1, 8):
            pivots = jnp.where(row_index == k, columns[k][s], pivots)
        own = tiles[s]
        for k in range(8):
            pivot_row = spread_row(own, k)
            own = own - multipliers[k][s] * pivot_row
            for i in range(s + 1, count):
                tiles[i] = tiles[i] - multipliers[k][i] * pivot_row
        tiles[s] = own * lax.rsqrt(pivots)
    return tiles


def invert_factor(gram, work_ref, inverse_ref):
    rows = lax.broadcasted_iota(jnp.int32, (RANK, RANK), 0)
    lanes = lax.broadcasted_iota(jnp.int32, (RANK, RANK), 1)
    diagonal = rows == lanes
    ridge = (1e-06 / RANK) * jnp.sum(jnp.where(diagonal, gram, 0.0), keepdims=True)
    work_ref[:, :RANK] = gram + jnp.where(diagonal, ridge, 0.0)
    work_ref[:, RANK:] = jnp.where(diagonal, 1.0, 0.0)
    row_index = lax.broadcasted_iota(jnp.int32, (8, 128), 0)
    lane_index = lax.broadcasted_iota(jnp.int32, (8, 128), 1)
    for block in range(RANK // BLOCK):
        top = block * BLOCK
        aligned = top // 128 * 128
        first_lane = top - aligned
        own_half = lane_index >= 64 if first_lane else lane_index < 64
        tiles = []
        for i in range(BLOCK // 8):
            part = work_ref[top + 8 * i : top + 8 * i + 8, aligned : aligned + 128]
            unit = jnp.where(lane_index == row_index + (8 * i + 64 - first_lane), 1.0, 0.0)
            tiles.append(jnp.where(own_half, part, unit))
        factored = jnp.concatenate(factor_block(tiles, first_lane, row_index), axis=0)
        if first_lane == 0:
            factored = pltpu.roll(factored, 64, 1)
        done = multiply(factored[:, :BLOCK], work_ref[top : top + BLOCK, :], 1, 0)
        inverse_ref[top : top + BLOCK, :] = done[:, RANK:]
        if top + BLOCK < RANK:
            below = top + BLOCK
            start = below // 128 * 128
            update = multiply(done[:, start:RANK], done, 0, 0)
            work_ref[below:, :] = work_ref[below:, :] - update[below - start :, :]


def split_multiply(left_side, right_side):
    def halves(value):
        high = value.astype(jnp.bfloat16)
        return high, (value - high.astype(jnp.float32)).astype(jnp.bfloat16)

    def part(a, b):
        return multiply(a, b, 1, 0, None)

    left_high, left_low = halves(left_side)
    right_high, right_low = halves(right_side)
    return part(left_high, right_high) + (
        part(left_high, right_low) + part(left_low, right_high)
    )


def first_kernel(
    place_ref, gram_ref, left_ref, momentum_ref, gradient_ref,
    once_ref, kept_ref, given_ref, work_ref, inverse_ref, square_ref, right_ref,
    held_momentum, held_gradient, arrived,
):
    quarter, core = place_ref[0], place_ref[1]
    fetches = (
        pltpu.make_async_copy(momentum_ref, held_momentum, arrived.at[0]),
        pltpu.make_async_copy(gradient_ref, held_gradient, arrived.at[1]),
    )
    for fetch in fetches:
        fetch.start()
    invert_factor(gram_ref[...], work_ref, inverse_ref)
    once = multiply(left_ref[...], inverse_ref[...], 1, 1)
    once_ref[...] = once
    turned = once.T
    square_ref[...] = multiply(turned, turned, 1, 1)
    for fetch in fetches:
        fetch.wait()
    buffer = held_momentum[...] + held_gradient[...].astype(jnp.float32)
    right_ref[...] = multiply(turned, buffer, 1, 0)
    for target, half in ((kept_ref, core), (given_ref, 1 - core)):
        target[:HALF, :] = right_ref[pl.ds(pl.multiple_of(half * HALF, HALF), HALF), :]
        start = pl.multiple_of(quarter * 64 + half * 32, 32)
        for i in range(4):
            target[HALF + 8 * i : HALF + 8 * i + 8, :RANK] = square_ref[pl.ds(start + 8 * i, 8), :]
        target[HALF:, RANK:] = jnp.zeros((32, target.shape[1] - RANK), jnp.float32)


def second_kernel(
    place_ref, own_ref, other_ref, once_ref, inverse_ref, basis_ref, gram_ref, work_ref,
    held_once, arrived,
):
    quarter, core = place_ref[0], place_ref[1]
    fetch = pltpu.make_async_copy(once_ref, held_once, arrived.at[0])
    fetch.start()
    for step in range(4):
        base = lax.rem(quarter + (4 - step), 4) * 64
        for source, half in ((own_ref, core), (other_ref, 1 - core)):
            start = pl.multiple_of(base + half * 32, 32)
            gram_ref[pl.ds(start, 32), :] = source[32 * step : 32 * step + 32, :]
    invert_factor(gram_ref[...], work_ref, inverse_ref)
    fetch.wait()
    basis_ref[...] = multiply(held_once[...], inverse_ref[...], 1, 1)


def third_kernel(place_ref, own_ref, other_ref, inverse_ref, right_ref, square_ref, whole_ref):
    core = place_ref[1]
    for source, half in ((own_ref, core), (other_ref, 1 - core)):
        whole_ref[pl.ds(pl.multiple_of(half * HALF, HALF), HALF), :] = source[...]
    right = multiply(inverse_ref[...], whole_ref[...], 1, 0)
    right_ref[...] = right
    ones = jnp.ones((8, right.shape[1]), jnp.float32)
    square_ref[...] = multiply(ones, right * right, 1, 1)


def fourth_kernel(
    momentum_ref, gradient_ref, basis_ref, right_ref, next_ref, turned_ref,
    held_momentum, held_gradient, arrived,
):
    fetches = (
        pltpu.make_async_copy(momentum_ref, held_momentum, arrived.at[0]),
        pltpu.make_async_copy(gradient_ref, held_gradient, arrived.at[1]),
    )
    for fetch in fetches:
        fetch.start()
    turned_ref[...] = right_ref[...].T
    product = split_multiply(basis_ref[...], right_ref[...])
    for fetch in fetches:
        fetch.wait()
    buffer = held_momentum[...] + held_gradient[...].astype(jnp.float32)
    next_ref[...] = buffer - error_share * product


def fifth_kernel(squares_ref, basis_ref, right_ref, turned_ref, next_ref, step_ref):
    square_sum = squares_ref[0]
    for i in range(1, TENSOR):
        square_sum = square_sum + squares_ref[i]
    scale = lax.rsqrt(square_sum * (1.0 / FFW) + 1e-06)
    next_ref[...] = turned_ref[...] * scale
    scaled = basis_ref[...] * (scale * math.sqrt(D / RANK))
    step_ref[...] = split_multiply(scaled, right_ref[...])


def sum_kernel(parts_ref, copies_ref, rest_ref=None):
    count = parts_ref.shape[0]
    total = parts_ref[0]
    for i in range(1, count):
        total = total + parts_ref[i]
    width = copies_ref.shape[2]
    for i in range(copies_ref.shape[0]):
        copies_ref[i] = total[:, :width]
    if rest_ref is not None:
        height = total.shape[0]
        for i in range(rest_ref.shape[0] // height):
            start = width + i * RANK
            rest_ref[i * height : (i + 1) * height, :] = total[:, start : start + RANK]


def call(kernel, name, operands, outputs, scratch=(), far=(), scalars=True):
    specs = [pl.BlockSpec(memory_space=pltpu.VMEM)] * len(operands)
    if scalars:
        specs[0] = pl.BlockSpec(memory_space=pltpu.SMEM)
    for i in far:
        specs[i] = pl.BlockSpec(memory_space=pl.ANY)
    held = [pltpu.VMEM(operands[i].shape, operands[i].dtype) for i in far]
    arrived = [pltpu.SemaphoreType.DMA((len(far),))] if far else []
    return pl.pallas_call(
        kernel,
        out_shape=[jax.ShapeDtypeStruct(shape, jnp.float32) for shape in outputs],
        in_specs=specs,
        out_specs=[pl.BlockSpec(memory_space=pltpu.VMEM)] * len(outputs),
        scratch_shapes=[pltpu.VMEM(shape, jnp.float32) for shape in scratch] + held + arrived,
        compiler_params=pltpu.CompilerParams(vmem_limit_bytes=VMEM),
        cost_estimate=pl.CostEstimate(
            flops=10**9, bytes_accessed=8 * 2**20, transcendentals=0
        ),
        name=name,
    )(*operands)


plane_groups = [
    [(2 * z + core) * TENSOR + t for t in range(TENSOR) for core in range(2)] for z in range(Z)
]
both_axes = ("fsdp", "tensor")


def exchange(block, axis, groups=None):
    return lax.all_to_all(block, axis, 0, 0, axis_index_groups=groups, tiled=True)


def copies(block, members):
    return jnp.broadcast_to(block, (members,) + block.shape)


def swap_cores(block):
    return lax.ppermute(block, "fsdp", [(i, i ^ 1) for i in range(2 * Z)])


def core_half(block, core):
    half = block.shape[0] // 2
    kept = lax.dynamic_slice_in_dim(block, core * half, half)
    given = lax.dynamic_slice_in_dim(block, (1 - core) * half, half)
    return kept + swap_cores(given)


def gram_rows(factor, place):
    width = RANK // TENSOR
    own = lax.dynamic_slice_in_dim(factor, place * width, width, axis=1)
    return multiply(own, factor, 0, 0)


def per_device(momentum, gradient, right_state):
    core = lax.axis_index("fsdp") % 2
    place = lax.axis_index("tensor")
    where = jnp.stack([place % 4, core]).astype(jnp.int32)
    buffer = momentum + gradient.astype(jnp.float32)
    partial_left = multiply(buffer, right_state, 1, 0)
    rows, columns = buffer.shape
    parts = exchange(partial_left.reshape(TENSOR, rows // TENSOR, RANK), "tensor")
    (parts,) = call(sum_kernel, "left_sum", (parts,), (parts.shape,), scalars=False)
    left_raw = exchange(parts, "tensor").reshape(rows, RANK)

    gram_part = core_half(gram_rows(left_raw, place), core)
    parts = exchange(copies(gram_part, Z), "fsdp", z_groups)
    (parts,) = call(
        sum_kernel, "gram_sum", (parts,), ((2 * TENSOR,) + parts.shape[1:],), scalars=False
    )
    gram = exchange(parts, both_axes, plane_groups).reshape(RANK, RANK)
    left_once, kept, given = call(
        first_kernel,
        "first",
        (where, gram, left_raw, momentum, gradient),
        ((rows, RANK), (HALF + 32, columns), (HALF + 32, columns)),
        ((RANK, 2 * RANK), (RANK, RANK), (RANK, RANK), (RANK, columns)),
        far=(3, 4),
    )

    part = kept + swap_cores(given)
    piece = HALF // Z
    gram_part = part[HALF:, :RANK]
    gram_part = jnp.concatenate([gram_part[:piece], gram_part[piece:]], axis=1)
    parts = jnp.concatenate(
        [part[:HALF].reshape(Z, piece, columns), copies(gram_part, Z)], axis=2
    )
    parts = exchange(parts, "fsdp", z_groups)
    parts, gram_part = call(
        sum_kernel, "right_sum", (parts,), ((Z, piece, columns), (32, RANK)), scalars=False
    )
    right_part = exchange(parts, "fsdp", z_groups)
    received = [gram_part]
    for step in range(1, 4):
        pairs = [(i, i // 4 * 4 + (i + step) % 4) for i in range(TENSOR)]
        received.append(lax.ppermute(gram_part, "tensor", pairs))
    gram_part = jnp.concatenate(received, axis=0)
    inverse, left_basis = call(
        second_kernel,
        "second",
        (where, gram_part, swap_cores(gram_part), left_once),
        ((RANK, RANK), (rows, RANK)),
        ((RANK, RANK), (RANK, 2 * RANK)),
        far=(3,),
    )
    right_part, inverse = lax.optimization_barrier((right_part, inverse))
    right_part = right_part.reshape(HALF, columns)
    right_factor, square_sum = call(
        third_kernel,
        "third",
        (where, right_part, swap_cores(right_part), inverse),
        ((RANK, columns), (8, RANK)),
        ((RANK, columns),),
    )
    square_sum = exchange(copies(square_sum[:1], TENSOR), "tensor")
    momentum_next, turned = call(
        fourth_kernel,
        "fourth",
        (momentum, gradient, left_basis, right_factor),
        ((rows, columns), (columns, RANK)),
        far=(0, 1),
        scalars=False,
    )
    right_next, step_direction = call(
        fifth_kernel,
        "fifth",
        (square_sum, left_basis, right_factor, turned),
        ((columns, RANK), (rows, columns)),
        scalars=False,
    )
    return (momentum_next, right_next, step_direction)


def solution(mesh):
    return jax.shard_map(
        per_device,
        mesh=mesh,
        in_specs=(P("fsdp", "tensor"), P("fsdp", "tensor"), P("tensor", None)),
        out_specs=(P("fsdp", "tensor"), P("tensor", None), P("fsdp", "tensor")),
        check_vma=False,
    )
```

```python
import math

import jax
import jax.numpy as jnp
from jax import lax
from jax.experimental import pallas as pl
from jax.experimental.pallas import tpu as pltpu
from jax.sharding import PartitionSpec as P

D = 8192
FFW = 14336
RANK = 256
BLOCK = 64
HALF = RANK // 2
VMEM = 20 * 2**20
TENSOR = 16
Z = 8

highest = lax.Precision.HIGHEST
error_share = 0.05
z_groups = [[2 * z + core for z in range(Z)] for core in range(2)]


def multiply(left_side, right_side, left_dim, right_dim, precision=highest):
    return lax.dot_general(
        left_side,
        right_side,
        (((left_dim,), (right_dim,)), ((), ())),
        precision=precision,
        preferred_element_type=jnp.float32,
    )


def spread_lane(tile, lane):
    return jnp.take_along_axis(tile, jnp.full(tile.shape, lane, jnp.int32), axis=1)


def spread_row(tile, row):
    return jnp.broadcast_to(tile[row : row + 1, :], tile.shape)


def factor_block(tiles, first_lane, row_index):
    tiles = list(tiles)
    count = len(tiles)
    for s in range(count):
        columns = [
            {i: spread_lane(tiles[i], first_lane + 8 * s + j) for i in range(s, count)}
            for j in range(8)
        ]
        multipliers = []
        for k in range(8):
            inverse_pivot = 1.0 / spread_row(columns[k][s], k)
            multiplier = {i: columns[k][i] * inverse_pivot for i in range(s, count)}
            below = jnp.where(row_index > k, multiplier[s], 0.0)
            multipliers.append({**multiplier, s: below})
            for j in range(k + 1, 8):
                pivot_row = spread_row(columns[j][s], k)
                for i in range(s, count):
                    columns[j][i] = columns[j][i] - multiplier[i] * pivot_row
        pivots = columns[0][s]
        for k in range(1, 8):
            pivots = jnp.where(row_index == k, columns[k][s], pivots)
        own = tiles[s]
        for k in range(8):
            pivot_row = spread_row(own, k)
            own = own - multipliers[k][s] * pivot_row
            for i in range(s + 1, count):
                tiles[i] = tiles[i] - multipliers[k][i] * pivot_row
        tiles[s] = own * lax.rsqrt(pivots)
    return tiles


def invert_factor(gram, work_ref, inverse_ref):
    rows = lax.broadcasted_iota(jnp.int32, (RANK, RANK), 0)
    lanes = lax.broadcasted_iota(jnp.int32, (RANK, RANK), 1)
    diagonal = rows == lanes
    ridge = (1e-06 / RANK) * jnp.sum(jnp.where(diagonal, gram, 0.0), keepdims=True)
    work_ref[:, :RANK] = gram + jnp.where(diagonal, ridge, 0.0)
    work_ref[:, RANK:] = jnp.where(diagonal, 1.0, 0.0)
    row_index = lax.broadcasted_iota(jnp.int32, (8, 128), 0)
    lane_index = lax.broadcasted_iota(jnp.int32, (8, 128), 1)
    for block in range(RANK // BLOCK):
        top = block * BLOCK
        aligned = top // 128 * 128
        first_lane = top - aligned
        own_half = lane_index >= 64 if first_lane else lane_index < 64
        tiles = []
        for i in range(BLOCK // 8):
            part = work_ref[top + 8 * i : top + 8 * i + 8, aligned : aligned + 128]
            unit = jnp.where(lane_index == row_index + (8 * i + 64 - first_lane), 1.0, 0.0)
            tiles.append(jnp.where(own_half, part, unit))
        factored = jnp.concatenate(factor_block(tiles, first_lane, row_index), axis=0)
        if first_lane == 0:
            factored = pltpu.roll(factored, 64, 1)
        done = multiply(factored[:, :BLOCK], work_ref[top : top + BLOCK, :], 1, 0)
        inverse_ref[top : top + BLOCK, :] = done[:, RANK:]
        if top + BLOCK < RANK:
            below = top + BLOCK
            start = below // 128 * 128
            update = multiply(done[:, start:RANK], done, 0, 0)
            work_ref[below:, :] = work_ref[below:, :] - update[below - start :, :]


def terms(value, count):
    found = []
    for left in range(count - 1, -1, -1):
        term = value.astype(jnp.bfloat16)
        found.append(term)
        if left:
            value = value - term.astype(jnp.float32)
    return found


CHUNKS = 4


def term_multiply(left_terms, right_terms, right_dim=0):
    count = len(right_terms)
    rows = left_terms[0].shape[0]
    total = None
    for order in range(count - 1, -1, -1):
        met = left_terms[: count - order]
        stack = met[0] if len(met) == 1 else jnp.concatenate(met, axis=0)
        product = multiply(stack, right_terms[order], 1, right_dim, None)
        for i in range(len(met) - 1, -1, -1):
            part = product[i * rows : (i + 1) * rows]
            total = part if total is None else total + part
    return total


def pack_gram(rows, quarter, row_lane):
    turned = rows
    for i in range(1, 4):
        turned = jnp.where(quarter == i, pltpu.roll(rows, RANK - 64 * i, 1), turned)
    tiles = [turned[8 * i : 8 * i + 8, :128] for i in range(4)]
    for i in (0, 2):
        first, second = (turned[8 * k : 8 * k + 8, 128:] for k in (i, i + 1))
        tiles.append(jnp.where(row_lane < 64, first, pltpu.roll(second, 64, 1)))
    return tiles


def unpack_gram(tiles, row_lane):
    rows = []
    for i in range(4):
        near = tiles[i] * jnp.where(row_lane < 64, 0.5, 1.0)
        far = tiles[4 + i // 2]
        far = pltpu.roll(far, 64, 1) if i % 2 else far
        rows.append(jnp.concatenate([near, jnp.where(row_lane < 64, 0.5 * far, 0.0)], axis=1))
    return rows


def first_kernel(
    place_ref, gram_ref, left_ref, momentum_ref, gradient_ref,
    once_ref, kept_ref, given_ref, work_ref, inverse_ref, square_ref, right_ref,
    held_momentum, held_gradient, arrived,
):
    quarter, core = place_ref[0], place_ref[1]
    fetches = (
        pltpu.make_async_copy(momentum_ref, held_momentum, arrived.at[0]),
        pltpu.make_async_copy(gradient_ref, held_gradient, arrived.at[1]),
    )
    for fetch in fetches:
        fetch.start()
    invert_factor(gram_ref[...], work_ref, inverse_ref)
    once = multiply(left_ref[...], inverse_ref[...], 1, 1)
    once_ref[...] = once
    turned = terms(once.T, 3)
    square_ref[...] = term_multiply(turned, turned, 1)
    for fetch in fetches:
        fetch.wait()
    buffer = held_momentum[...] + held_gradient[...].astype(jnp.float32)
    right_ref[...] = term_multiply(turned, terms(buffer, 3))
    row_lane = lax.broadcasted_iota(jnp.int32, (8, 128), 1)
    for target, half in ((kept_ref, core), (given_ref, 1 - core)):
        target[:HALF, :] = right_ref[pl.ds(pl.multiple_of(half * HALF, HALF), HALF), :]
        start = pl.multiple_of(quarter * 64 + half * 32, 32)
        tiles = pack_gram(square_ref[pl.ds(start, 32), :], quarter, row_lane)
        for i, tile in enumerate(tiles):
            target[HALF:, 128 * i : 128 * i + 128] = tile
        target[HALF:, 768:] = jnp.zeros((8, target.shape[1] - 768), jnp.float32)


def second_kernel(place_ref, own_ref, other_ref, once_ref, found_ref, gram_ref, work_ref):
    rows = once_ref.shape[0]
    inverse_ref = found_ref.at[rows:]
    quarter, core = place_ref[0], place_ref[1]
    row_lane = lax.broadcasted_iota(jnp.int32, (8, 128), 1)
    for step in range(4):
        base = lax.rem(quarter + (4 - step), 4) * 64
        for source, half in ((own_ref, core), (other_ref, 1 - core)):
            tiles = [
                source[16 * step + top : 16 * step + top + 8, 128 * i : 128 * i + 128]
                for top in (0, 8)
                for i in range(3)
            ]
            start = pl.multiple_of(base + half * 32, 32)
            for i, part in enumerate(unpack_gram(tiles, row_lane)):
                gram_ref[pl.ds(start + 8 * i, 8), :] = part
    parts = [gram_ref[64 * i : 64 * i + 64, :] for i in range(4)]
    parts = [parts[0]] + [pltpu.roll(parts[i], 64 * i, 1) for i in range(1, 4)]
    gram = jnp.concatenate(parts, axis=0)
    invert_factor(gram + gram.T, work_ref, inverse_ref)
    found_ref[:rows, :] = multiply(once_ref[...], inverse_ref[...], 1, 1)


def third_kernel(place_ref, own_ref, other_ref, found_ref, right_ref, square_ref, whole_ref):
    core = place_ref[1]
    for source, half in ((own_ref, core), (other_ref, 1 - core)):
        whole_ref[pl.ds(pl.multiple_of(half * HALF, HALF), HALF), :] = source[...]
    inverse = found_ref[found_ref.shape[0] - RANK :, :]
    right = multiply(inverse, whole_ref[...], 1, 0)
    right_ref[...] = right
    squares = right[:, :128] * right[:, :128]
    for start in range(128, right.shape[1], 128):
        part = right[:, start : start + 128]
        squares = squares + part * part
    squares = jnp.sum(squares.T, axis=0, keepdims=True)
    for i in range(TENSOR):
        square_ref[i] = squares


def fourth_kernel(
    momentum_ref, gradient_ref, found_ref, right_ref,
    next_ref, turned_ref, held_momentum, held_gradient, arrived,
):
    fetches = (
        pltpu.make_async_copy(momentum_ref, held_momentum, arrived.at[0]),
        pltpu.make_async_copy(gradient_ref, held_gradient, arrived.at[1]),
    )
    for fetch in fetches:
        fetch.start()
    turned_ref[...] = right_ref[...].T
    basis = found_ref[: next_ref.shape[0], :]
    product = term_multiply(terms(basis, 2), terms(right_ref[...], 2))
    for fetch in fetches:
        fetch.wait()
    buffer = held_momentum[...] + held_gradient[...].astype(jnp.float32)
    next_ref[...] = buffer - error_share * product


def fifth_kernel(
    squares_ref, found_ref, right_ref, turned_ref, next_ref, step_ref,
    next_held, step_held, done,
):
    square_sum = squares_ref[0]
    for i in range(1, TENSOR):
        square_sum = square_sum + squares_ref[i]
    scale = lax.rsqrt(square_sum * (1.0 / FFW) + 1e-06)
    next_held[...] = turned_ref[...] * scale
    writes = [pltpu.make_async_copy(next_held, next_ref, done.at[CHUNKS])]
    writes[0].start()
    rows, width = step_held.shape
    left = terms(found_ref[:rows, :] * (scale * math.sqrt(D / RANK)), 2)
    for i, start in enumerate(range(0, width, RANK)):
        columns = pl.ds(start, min(RANK, width - start))
        step_held[:, columns] = term_multiply(left, terms(right_ref[:, columns], 2))
        writes.append(pltpu.make_async_copy(step_held.at[:, columns], step_ref.at[:, columns], done.at[i]))
        writes[-1].start()
    for write in writes:
        write.wait()


def sum_kernel(parts_ref, copies_ref, rest_ref=None):
    total = parts_ref[0]
    for i in range(1, parts_ref.shape[0]):
        total = total + parts_ref[i]
    width = copies_ref.shape[2]
    for i in range(copies_ref.shape[0]):
        copies_ref[i] = total[:, :width]
    if rest_ref is not None:
        rest_ref[...] = total[:, width:]


def call(kernel, name, operands, outputs, scratch=(), far=(), scalars=True, near=(), out_far=()):
    operands = list(operands)
    in_specs = [pl.BlockSpec(memory_space=pltpu.VMEM)] * len(operands)
    if scalars:
        in_specs[0] = pl.BlockSpec(memory_space=pltpu.SMEM)
    for i in far:
        operands[i] = pltpu.with_memory_space_constraint(operands[i], pltpu.HBM)
        in_specs[i] = pl.BlockSpec(memory_space=pl.ANY)
    out_shape, out_specs = [], []
    for i, output in enumerate(outputs):
        shape, dtype = output if isinstance(output[0], tuple) else (output, jnp.float32)
        out_shape.append(
            pltpu.VMEM(shape, dtype) if i in near else jax.ShapeDtypeStruct(shape, dtype)
        )
        space = pl.ANY if i in out_far else pltpu.VMEM
        out_specs.append(pl.BlockSpec(memory_space=space))
    return pl.pallas_call(
        kernel,
        out_shape=out_shape,
        in_specs=in_specs,
        out_specs=out_specs,
        scratch_shapes=list(scratch),
        compiler_params=pltpu.CompilerParams(vmem_limit_bytes=VMEM),
        cost_estimate=pl.CostEstimate(
            flops=10**9, bytes_accessed=8 * 2**20, transcendentals=0
        ),
        name=name,
    )(*operands)


def room(*shape, dtype=jnp.float32):
    return pltpu.VMEM(shape, dtype)


plane_groups = [
    [(2 * z + core) * TENSOR + t for t in range(TENSOR) for core in range(2)] for z in range(Z)
]
both_axes = ("fsdp", "tensor")


def exchange(block, axis, groups=None):
    return lax.all_to_all(block, axis, 0, 0, axis_index_groups=groups, tiled=True)


def copies(block, members):
    return jnp.broadcast_to(block, (members,) + block.shape)


def swap_cores(block):
    return lax.ppermute(block, "fsdp", [(i, i ^ 1) for i in range(2 * Z)])


def core_half(block, core):
    half = block.shape[0] // 2
    kept = lax.dynamic_slice_in_dim(block, core * half, half)
    given = lax.dynamic_slice_in_dim(block, (1 - core) * half, half)
    return kept + swap_cores(given)


def gram_rows(factor, place):
    width = RANK // TENSOR
    own = lax.dynamic_slice_in_dim(factor, place * width, width, axis=1)
    return multiply(own, factor, 0, 0)


def per_device(momentum, gradient, right_state):
    core = lax.axis_index("fsdp") % 2
    place = lax.axis_index("tensor")
    where = jnp.stack([place % 4, core]).astype(jnp.int32)
    rows, columns = momentum.shape
    held = [room(rows, columns), room(rows, columns, dtype=gradient.dtype)]
    partial_left = multiply(momentum + gradient.astype(jnp.float32), right_state, 1, 0)
    parts = exchange(partial_left.reshape(TENSOR, rows // TENSOR, RANK), "tensor")
    (parts,) = call(sum_kernel, "left_sum", (parts,), (parts.shape,), scalars=False)
    left_raw = exchange(parts, "tensor").reshape(rows, RANK)

    gram_part = core_half(gram_rows(left_raw, place), core)
    parts = exchange(copies(gram_part, Z), "fsdp", z_groups)
    (parts,) = call(
        sum_kernel, "gram_sum", (parts,), ((2 * TENSOR,) + parts.shape[1:],), scalars=False
    )
    gram = exchange(parts, both_axes, plane_groups).reshape(RANK, RANK)
    work = [room(RANK, 2 * RANK), room(RANK, RANK)]
    left_once, kept, given = call(
        first_kernel,
        "first",
        (where, gram, left_raw, momentum, gradient),
        ((rows, RANK), (HALF + 8, columns), (HALF + 8, columns)),
        work + [room(RANK, RANK), room(RANK, columns)] + held + [pltpu.SemaphoreType.DMA((2,))],
        far=(3, 4),
        near=(0,),
    )

    part = kept + swap_cores(given)
    piece = HALF // Z
    gram_part = jnp.concatenate([part[HALF:, :384], part[HALF:, 384:768]], axis=0)
    parts = jnp.concatenate(
        [part[:HALF].reshape(Z, piece, columns), copies(gram_part, Z)], axis=2
    )
    parts = exchange(parts, "fsdp", z_groups)
    parts, gram_part = call(
        sum_kernel, "right_sum", (parts,), ((Z, piece, columns), (piece, 384)), scalars=False
    )
    right_part = exchange(parts, "fsdp", z_groups)
    received = [gram_part]
    for step in range(1, 4):
        pairs = [(i, i // 4 * 4 + (i + step) % 4) for i in range(TENSOR)]
        received.append(lax.ppermute(gram_part, "tensor", pairs))
    gram_part = jnp.concatenate(received, axis=0)
    (found,) = call(
        second_kernel,
        "second",
        (where, gram_part, swap_cores(gram_part), left_once),
        ((rows + RANK, RANK),),
        (work[1], work[0]),
        near=(0,),
    )
    right_part, found = lax.optimization_barrier((right_part, found))
    right_part = right_part.reshape(HALF, columns)
    right_factor, square_sum = call(
        third_kernel,
        "third",
        (where, right_part, swap_cores(right_part), found),
        ((RANK, columns), (TENSOR, 1, RANK)),
        [room(RANK, columns)],
        near=(0,),
    )
    square_sum = exchange(square_sum, "tensor")
    momentum_next, turned = call(
        fourth_kernel,
        "fourth",
        (momentum, gradient, found, right_factor),
        ((rows, columns), (columns, RANK)),
        held + [pltpu.SemaphoreType.DMA((2,))],
        far=(0, 1),
        scalars=False,
        near=(1,),
    )
    right_next, step_direction = call(
        fifth_kernel,
        "fifth",
        (square_sum, found, right_factor, turned),
        ((columns, RANK), (rows, columns)),
        [room(columns, RANK), room(rows, columns), pltpu.SemaphoreType.DMA((CHUNKS + 1,))],
        scalars=False,
        out_far=(0, 1),
    )
    return (momentum_next, right_next, step_direction)


def solution(mesh):
    return jax.shard_map(
        per_device,
        mesh=mesh,
        in_specs=(P("fsdp", "tensor"), P("fsdp", "tensor"), P("tensor", None)),
        out_specs=(P("fsdp", "tensor"), P("tensor", None), P("fsdp", "tensor")),
        check_vma=False,
    )
```

```python
import math

import jax
import jax.numpy as jnp
from jax import lax
from jax.experimental import pallas as pl
from jax.experimental.pallas import tpu as pltpu
from jax.sharding import PartitionSpec as P

D = 8192
FFW = 14336
RANK = 256
BLOCK = 64
HALF = RANK // 2
VMEM = 20 * 2**20
TENSOR = 16
Z = 8

highest = lax.Precision.HIGHEST
error_share = 0.05
z_groups = [[2 * z + core for z in range(Z)] for core in range(2)]


def multiply(left_side, right_side, left_dim, right_dim, precision=highest):
    return lax.dot_general(
        left_side,
        right_side,
        (((left_dim,), (right_dim,)), ((), ())),
        precision=precision,
        preferred_element_type=jnp.float32,
    )


def spread_lane(tile, lane):
    return jnp.take_along_axis(tile, jnp.full(tile.shape, lane, jnp.int32), axis=1)


def spread_row(tile, row):
    return jnp.broadcast_to(tile[row : row + 1, :], tile.shape)


def factor_block(tiles, first_lane, row_index):
    tiles = list(tiles)
    count = len(tiles)
    own = [spread_lane(tiles[0], first_lane + j) for j in range(8)]
    for s in range(count):
        below = range(s + 1, count)
        columns = [
            {i: spread_lane(tiles[i], first_lane + 8 * s + j) for i in below} for j in range(8)
        ]
        if below:
            following = [
                spread_lane(tiles[s + 1], first_lane + 8 * (s + 1) + j) for j in range(8)
            ]
        steps, own_steps, pivots = [], [], None
        for k in range(8):
            pivot = spread_row(own[k], k)
            inverse_pivot = 1.0 / pivot
            pivots = pivot if pivots is None else jnp.where(row_index == k, pivot, pivots)
            own_step = own[k] * inverse_pivot
            step = {i: columns[k][i] * inverse_pivot for i in below}
            own_steps.append(jnp.where(row_index > k, own_step, 0.0))
            steps.append(step)
            for j in range(k + 1, 8):
                entry = spread_row(own[j], k)
                own[j] = own[j] - own_step * entry
                for i in below:
                    columns[j][i] = columns[j][i] - step[i] * entry
            if below:
                for j in range(8):
                    following[j] = following[j] - step[s + 1] * spread_row(columns[k][s + 1], j)
        tile = tiles[s]
        for k in range(8):
            pivot_row = spread_row(tile, k)
            tile = tile - own_steps[k] * pivot_row
            for i in below:
                tiles[i] = tiles[i] - steps[k][i] * pivot_row
        tiles[s] = tile * lax.rsqrt(pivots)
        own = following
    return tiles


def deep_multiply(left_side, right_side):
    high, middle, low = terms(left_side, 3)
    left = jnp.concatenate([low, high, middle, middle, high, high], axis=1)
    high, middle, low = terms(right_side, 3)
    right = jnp.concatenate([high, low, middle, high, middle, high], axis=0)
    return multiply(left, right, 1, 0, None)


def invert_factor(gram, work_ref, inverse_ref):
    rows = lax.broadcasted_iota(jnp.int32, (RANK, RANK), 0)
    lanes = lax.broadcasted_iota(jnp.int32, (RANK, RANK), 1)
    diagonal = rows == lanes
    ridge = (1e-06 / RANK) * jnp.sum(jnp.where(diagonal, gram, 0.0), keepdims=True)
    work_ref[:, :RANK] = gram + jnp.where(diagonal, ridge, 0.0)
    work_ref[:, RANK:] = jnp.where(diagonal, 1.0, 0.0)
    row_index = lax.broadcasted_iota(jnp.int32, (8, 128), 0)
    lane_index = lax.broadcasted_iota(jnp.int32, (8, 128), 1)
    for block in range(RANK // BLOCK):
        top = block * BLOCK
        aligned = top // 128 * 128
        first_lane = top - aligned
        own_half = lane_index >= 64 if first_lane else lane_index < 64
        tiles = []
        for i in range(BLOCK // 8):
            part = work_ref[top + 8 * i : top + 8 * i + 8, aligned : aligned + 128]
            unit = jnp.where(lane_index == row_index + (8 * i + 64 - first_lane), 1.0, 0.0)
            tiles.append(jnp.where(own_half, part, unit))
        factored = jnp.concatenate(factor_block(tiles, first_lane, row_index), axis=0)
        if first_lane == 0:
            factored = pltpu.roll(factored, 64, 1)
        below = top + BLOCK
        start = RANK if below == RANK else below // 128 * 128
        width = -(-below // 128) * 128
        stop = RANK + width
        done = deep_multiply(factored[:, :BLOCK], work_ref[top:below, start:stop])
        inverse_ref[top:below, :width] = done[:, RANK - start :]
        if width < RANK:
            inverse_ref[top:below, width:] = jnp.zeros((BLOCK, RANK - width), jnp.float32)
        if below < RANK:
            update = deep_multiply(done[:, : RANK - start].T, done)
            work_ref[below:, start:stop] = work_ref[below:, start:stop] - update[below - start :, :]


def terms(value, count):
    found = []
    for left in range(count - 1, -1, -1):
        term = value.astype(jnp.bfloat16)
        found.append(term)
        if left:
            value = value - term.astype(jnp.float32)
    return found


CHUNKS = 4


def term_multiply(left_terms, right_terms, right_dim=0):
    count = len(right_terms)
    rows = left_terms[0].shape[0]
    total = None
    for order in range(count - 1, -1, -1):
        met = left_terms[: count - order]
        stack = met[0] if len(met) == 1 else jnp.concatenate(met, axis=0)
        product = multiply(stack, right_terms[order], 1, right_dim, None)
        for i in range(len(met) - 1, -1, -1):
            part = product[i * rows : (i + 1) * rows]
            total = part if total is None else total + part
    return total


def pack_gram(rows, quarter, row_lane):
    turned = rows
    for i in range(1, 4):
        turned = jnp.where(quarter == i, pltpu.roll(rows, RANK - 64 * i, 1), turned)
    tiles = [turned[8 * i : 8 * i + 8, :128] for i in range(4)]
    for i in (0, 2):
        first, second = (turned[8 * k : 8 * k + 8, 128:] for k in (i, i + 1))
        tiles.append(jnp.where(row_lane < 64, first, pltpu.roll(second, 64, 1)))
    return tiles


def unpack_gram(tiles, row_lane):
    rows = []
    for i in range(4):
        near = tiles[i] * jnp.where(row_lane < 64, 0.5, 1.0)
        far = tiles[4 + i // 2]
        far = pltpu.roll(far, 64, 1) if i % 2 else far
        rows.append(jnp.concatenate([near, jnp.where(row_lane < 64, 0.5 * far, 0.0)], axis=1))
    return rows


def first_kernel(
    place_ref, gram_ref, left_ref, momentum_ref, gradient_ref,
    once_ref, kept_ref, given_ref, work_ref, inverse_ref, square_ref, right_ref,
    held_momentum, held_gradient, arrived,
):
    quarter, core = place_ref[0], place_ref[1]
    fetches = (
        pltpu.make_async_copy(momentum_ref, held_momentum, arrived.at[0]),
        pltpu.make_async_copy(gradient_ref, held_gradient, arrived.at[1]),
    )
    for fetch in fetches:
        fetch.start()
    invert_factor(gram_ref[...], work_ref, inverse_ref)
    once = multiply(left_ref[...], inverse_ref[...], 1, 1)
    once_ref[...] = once
    turned = terms(once.T, 3)
    square_ref[...] = term_multiply(turned, turned, 1)
    for fetch in fetches:
        fetch.wait()
    buffer = held_momentum[...] + held_gradient[...].astype(jnp.float32)
    right_ref[...] = term_multiply(turned, terms(buffer, 3))
    row_lane = lax.broadcasted_iota(jnp.int32, (8, 128), 1)
    for target, half in ((kept_ref, core), (given_ref, 1 - core)):
        target[:HALF, :] = right_ref[pl.ds(pl.multiple_of(half * HALF, HALF), HALF), :]
        start = pl.multiple_of(quarter * 64 + half * 32, 32)
        tiles = pack_gram(square_ref[pl.ds(start, 32), :], quarter, row_lane)
        for i, tile in enumerate(tiles):
            target[HALF:, 128 * i : 128 * i + 128] = tile
        target[HALF:, 768:] = jnp.zeros((8, target.shape[1] - 768), jnp.float32)


def second_kernel(place_ref, own_ref, other_ref, once_ref, found_ref, gram_ref, work_ref):
    rows = once_ref.shape[0]
    inverse_ref = found_ref.at[rows:]
    quarter, core = place_ref[0], place_ref[1]
    row_lane = lax.broadcasted_iota(jnp.int32, (8, 128), 1)
    for step in range(4):
        base = lax.rem(quarter + (4 - step), 4) * 64
        for source, half in ((own_ref, core), (other_ref, 1 - core)):
            tiles = [
                source[16 * step + top : 16 * step + top + 8, 128 * i : 128 * i + 128]
                for top in (0, 8)
                for i in range(3)
            ]
            start = pl.multiple_of(base + half * 32, 32)
            for i, part in enumerate(unpack_gram(tiles, row_lane)):
                gram_ref[pl.ds(start + 8 * i, 8), :] = part
    parts = [gram_ref[64 * i : 64 * i + 64, :] for i in range(4)]
    parts = [parts[0]] + [pltpu.roll(parts[i], 64 * i, 1) for i in range(1, 4)]
    gram = jnp.concatenate(parts, axis=0)
    invert_factor(gram + gram.T, work_ref, inverse_ref)
    found_ref[:rows, :] = multiply(once_ref[...], inverse_ref[...], 1, 1)


def third_kernel(place_ref, own_ref, other_ref, found_ref, right_ref, square_ref, whole_ref):
    core = place_ref[1]
    for source, half in ((own_ref, core), (other_ref, 1 - core)):
        whole_ref[pl.ds(pl.multiple_of(half * HALF, HALF), HALF), :] = source[...]
    inverse = found_ref[found_ref.shape[0] - RANK :, :]
    right = multiply(inverse, whole_ref[...], 1, 0)
    right_ref[...] = right
    squares = right[:, :128] * right[:, :128]
    for start in range(128, right.shape[1], 128):
        part = right[:, start : start + 128]
        squares = squares + part * part
    squares = jnp.sum(squares.T, axis=0, keepdims=True)
    for i in range(TENSOR):
        square_ref[i] = squares


def fourth_kernel(
    momentum_ref, gradient_ref, found_ref, right_ref,
    next_ref, turned_ref, held_momentum, held_gradient, arrived,
):
    fetches = (
        pltpu.make_async_copy(momentum_ref, held_momentum, arrived.at[0]),
        pltpu.make_async_copy(gradient_ref, held_gradient, arrived.at[1]),
    )
    for fetch in fetches:
        fetch.start()
    turned_ref[...] = right_ref[...].T
    basis = found_ref[: next_ref.shape[0], :]
    product = term_multiply(terms(basis, 2), terms(right_ref[...], 2))
    for fetch in fetches:
        fetch.wait()
    buffer = held_momentum[...] + held_gradient[...].astype(jnp.float32)
    next_ref[...] = buffer - error_share * product


def fifth_kernel(
    squares_ref, found_ref, right_ref, turned_ref, next_ref, step_ref,
    next_held, step_held, done,
):
    square_sum = squares_ref[0]
    for i in range(1, TENSOR):
        square_sum = square_sum + squares_ref[i]
    scale = lax.rsqrt(square_sum * (1.0 / FFW) + 1e-06)
    next_held[...] = turned_ref[...] * scale
    writes = [pltpu.make_async_copy(next_held, next_ref, done.at[CHUNKS])]
    writes[0].start()
    rows, width = step_held.shape
    left = terms(found_ref[:rows, :] * (scale * math.sqrt(D / RANK)), 2)
    for i, start in enumerate(range(0, width, RANK)):
        columns = pl.ds(start, min(RANK, width - start))
        step_held[:, columns] = term_multiply(left, terms(right_ref[:, columns], 2))
        writes.append(pltpu.make_async_copy(step_held.at[:, columns], step_ref.at[:, columns], done.at[i]))
        writes[-1].start()
    for write in writes:
        write.wait()


def sum_kernel(parts_ref, copies_ref, rest_ref=None):
    total = parts_ref[0]
    for i in range(1, parts_ref.shape[0]):
        total = total + parts_ref[i]
    width = copies_ref.shape[2]
    for i in range(copies_ref.shape[0]):
        copies_ref[i] = total[:, :width]
    if rest_ref is not None:
        rest_ref[...] = total[:, width:]


def call(kernel, name, operands, outputs, scratch=(), far=(), scalars=True, near=(), out_far=()):
    operands = list(operands)
    in_specs = [pl.BlockSpec(memory_space=pltpu.VMEM)] * len(operands)
    if scalars:
        in_specs[0] = pl.BlockSpec(memory_space=pltpu.SMEM)
    for i in far:
        operands[i] = pltpu.with_memory_space_constraint(operands[i], pltpu.HBM)
        in_specs[i] = pl.BlockSpec(memory_space=pl.ANY)
    out_shape, out_specs = [], []
    for i, output in enumerate(outputs):
        shape, dtype = output if isinstance(output[0], tuple) else (output, jnp.float32)
        out_shape.append(
            pltpu.VMEM(shape, dtype) if i in near else jax.ShapeDtypeStruct(shape, dtype)
        )
        space = pl.ANY if i in out_far else pltpu.VMEM
        out_specs.append(pl.BlockSpec(memory_space=space))
    return pl.pallas_call(
        kernel,
        out_shape=out_shape,
        in_specs=in_specs,
        out_specs=out_specs,
        scratch_shapes=list(scratch),
        compiler_params=pltpu.CompilerParams(vmem_limit_bytes=VMEM),
        cost_estimate=pl.CostEstimate(
            flops=10**9, bytes_accessed=8 * 2**20, transcendentals=0
        ),
        name=name,
    )(*operands)


def room(*shape, dtype=jnp.float32):
    return pltpu.VMEM(shape, dtype)


plane_groups = [
    [(2 * z + core) * TENSOR + t for t in range(TENSOR) for core in range(2)] for z in range(Z)
]
both_axes = ("fsdp", "tensor")


def exchange(block, axis, groups=None):
    return lax.all_to_all(block, axis, 0, 0, axis_index_groups=groups, tiled=True)


def copies(block, members):
    return jnp.broadcast_to(block, (members,) + block.shape)


def swap_cores(block):
    return lax.ppermute(block, "fsdp", [(i, i ^ 1) for i in range(2 * Z)])


def core_half(block, core):
    half = block.shape[0] // 2
    kept = lax.dynamic_slice_in_dim(block, core * half, half)
    given = lax.dynamic_slice_in_dim(block, (1 - core) * half, half)
    return kept + swap_cores(given)


def gram_rows(factor, place):
    width = RANK // TENSOR
    own = lax.dynamic_slice_in_dim(factor, place * width, width, axis=1)
    return multiply(own, factor, 0, 0)


def per_device(momentum, gradient, right_state):
    core = lax.axis_index("fsdp") % 2
    place = lax.axis_index("tensor")
    where = jnp.stack([place % 4, core]).astype(jnp.int32)
    rows, columns = momentum.shape
    held = [room(rows, columns), room(rows, columns, dtype=gradient.dtype)]
    partial_left = multiply(momentum + gradient.astype(jnp.float32), right_state, 1, 0)
    parts = exchange(partial_left.reshape(TENSOR, rows // TENSOR, RANK), "tensor")
    (parts,) = call(sum_kernel, "left_sum", (parts,), (parts.shape,), scalars=False)
    left_raw = exchange(parts, "tensor").reshape(rows, RANK)

    gram_part = core_half(gram_rows(left_raw, place), core)
    parts = exchange(copies(gram_part, Z), "fsdp", z_groups)
    (parts,) = call(
        sum_kernel, "gram_sum", (parts,), ((2 * TENSOR,) + parts.shape[1:],), scalars=False
    )
    gram = exchange(parts, both_axes, plane_groups).reshape(RANK, RANK)
    work = [room(RANK, 2 * RANK), room(RANK, RANK)]
    left_once, kept, given = call(
        first_kernel,
        "first",
        (where, gram, left_raw, momentum, gradient),
        ((rows, RANK), (HALF + 8, columns), (HALF + 8, columns)),
        work + [room(RANK, RANK), room(RANK, columns)] + held + [pltpu.SemaphoreType.DMA((2,))],
        far=(3, 4),
        near=(0,),
    )

    part = kept + swap_cores(given)
    piece = HALF // Z
    gram_part = jnp.concatenate([part[HALF:, :384], part[HALF:, 384:768]], axis=0)
    parts = jnp.concatenate(
        [part[:HALF].reshape(Z, piece, columns), copies(gram_part, Z)], axis=2
    )
    parts = exchange(parts, "fsdp", z_groups)
    parts, gram_part = call(
        sum_kernel, "right_sum", (parts,), ((Z, piece, columns), (piece, 384)), scalars=False
    )
    right_part = exchange(parts, "fsdp", z_groups)
    received = [gram_part]
    for step in range(1, 4):
        pairs = [(i, i // 4 * 4 + (i + step) % 4) for i in range(TENSOR)]
        received.append(lax.ppermute(gram_part, "tensor", pairs))
    gram_part = jnp.concatenate(received, axis=0)
    (found,) = call(
        second_kernel,
        "second",
        (where, gram_part, swap_cores(gram_part), left_once),
        ((rows + RANK, RANK),),
        (work[1], work[0]),
        near=(0,),
    )
    right_part, found = lax.optimization_barrier((right_part, found))
    right_part = right_part.reshape(HALF, columns)
    right_factor, square_sum = call(
        third_kernel,
        "third",
        (where, right_part, swap_cores(right_part), found),
        ((RANK, columns), (TENSOR, 1, RANK)),
        [room(RANK, columns)],
        near=(0,),
    )
    square_sum = exchange(square_sum, "tensor")
    momentum_next, turned = call(
        fourth_kernel,
        "fourth",
        (momentum, gradient, found, right_factor),
        ((rows, columns), (columns, RANK)),
        held + [pltpu.SemaphoreType.DMA((2,))],
        far=(0, 1),
        scalars=False,
        near=(1,),
    )
    right_next, step_direction = call(
        fifth_kernel,
        "fifth",
        (square_sum, found, right_factor, turned),
        ((columns, RANK), (rows, columns)),
        [room(columns, RANK), room(rows, columns), pltpu.SemaphoreType.DMA((CHUNKS + 1,))],
        scalars=False,
        out_far=(0, 1),
    )
    return (momentum_next, right_next, step_direction)


def solution(mesh):
    return jax.shard_map(
        per_device,
        mesh=mesh,
        in_specs=(P("fsdp", "tensor"), P("fsdp", "tensor"), P("tensor", None)),
        out_specs=(P("fsdp", "tensor"), P("tensor", None), P("fsdp", "tensor")),
        check_vma=False,
    )
```

```python
import math

import jax
import jax.numpy as jnp
from jax import lax
from jax.experimental import pallas as pl
from jax.experimental.pallas import tpu as pltpu
from jax.sharding import PartitionSpec as P

D = 8192
FFW = 14336
RANK = 256
BLOCK = 64
VMEM = 20 * 2**20
TENSOR = 16
Z = 8

highest = lax.Precision.HIGHEST
error_share = 0.05
z_groups = [[2 * z + core for z in range(Z)] for core in range(2)]


def multiply(left_side, right_side, left_dim, right_dim, precision=highest):
    return lax.dot_general(
        left_side,
        right_side,
        (((left_dim,), (right_dim,)), ((), ())),
        precision=precision,
        preferred_element_type=jnp.float32,
    )


def spread_lane(tile, lane):
    return jnp.take_along_axis(tile, jnp.full(tile.shape, lane, jnp.int32), axis=1)


def spread_row(tile, row):
    return jnp.broadcast_to(tile[row : row + 1, :], tile.shape)


def factor_block(tiles, first_lane, row_index):
    tiles = list(tiles)
    count = len(tiles)
    own = [spread_lane(tiles[0], first_lane + j) for j in range(8)]
    for s in range(count):
        below = range(s + 1, count)
        columns = [
            {i: spread_lane(tiles[i], first_lane + 8 * s + j) for i in below} for j in range(8)
        ]
        if below:
            following = [
                spread_lane(tiles[s + 1], first_lane + 8 * (s + 1) + j) for j in range(8)
            ]
        steps, own_steps, pivots = [], [], None
        for k in range(8):
            pivot = spread_row(own[k], k)
            inverse_pivot = 1.0 / pivot
            pivots = pivot if pivots is None else jnp.where(row_index == k, pivot, pivots)
            own_step = own[k] * inverse_pivot
            step = {i: columns[k][i] * inverse_pivot for i in below}
            own_steps.append(jnp.where(row_index > k, own_step, 0.0))
            steps.append(step)
            for j in range(k + 1, 8):
                entry = spread_row(own[j], k)
                own[j] = own[j] - own_step * entry
                for i in below:
                    columns[j][i] = columns[j][i] - step[i] * entry
            if below:
                for j in range(8):
                    following[j] = following[j] - step[s + 1] * spread_row(columns[k][s + 1], j)
        tile = tiles[s]
        for k in range(8):
            pivot_row = spread_row(tile, k)
            tile = tile - own_steps[k] * pivot_row
            for i in below:
                tiles[i] = tiles[i] - steps[k][i] * pivot_row
        tiles[s] = tile * lax.rsqrt(pivots)
        own = following
    return tiles


def deep_multiply(left_side, right_side):
    high, middle, low = terms(left_side, 3)
    left = jnp.concatenate([low, high, middle, middle, high, high], axis=1)
    high, middle, low = terms(right_side, 3)
    right = jnp.concatenate([high, low, middle, high, middle, high], axis=0)
    return multiply(left, right, 1, 0, None)


def invert_factor(gram, work_ref, inverse_ref):
    rows = lax.broadcasted_iota(jnp.int32, (RANK, RANK), 0)
    lanes = lax.broadcasted_iota(jnp.int32, (RANK, RANK), 1)
    diagonal = rows == lanes
    ridge = (1e-06 / RANK) * jnp.sum(jnp.where(diagonal, gram, 0.0), keepdims=True)
    work_ref[:, :RANK] = gram + jnp.where(diagonal, ridge, 0.0)
    work_ref[:, RANK:] = jnp.where(diagonal, 1.0, 0.0)
    row_index = lax.broadcasted_iota(jnp.int32, (8, 128), 0)
    lane_index = lax.broadcasted_iota(jnp.int32, (8, 128), 1)
    for block in range(RANK // BLOCK):
        top = block * BLOCK
        aligned = top // 128 * 128
        first_lane = top - aligned
        own_half = lane_index >= 64 if first_lane else lane_index < 64
        tiles = []
        for i in range(BLOCK // 8):
            part = work_ref[top + 8 * i : top + 8 * i + 8, aligned : aligned + 128]
            unit = jnp.where(lane_index == row_index + (8 * i + 64 - first_lane), 1.0, 0.0)
            tiles.append(jnp.where(own_half, part, unit))
        factored = jnp.concatenate(factor_block(tiles, first_lane, row_index), axis=0)
        if first_lane == 0:
            factored = pltpu.roll(factored, 64, 1)
        below = top + BLOCK
        start = RANK if below == RANK else below // 128 * 128
        width = -(-below // 128) * 128
        stop = RANK + width
        done = deep_multiply(factored[:, :BLOCK], work_ref[top:below, start:stop])
        inverse_ref[top:below, :width] = done[:, RANK - start :]
        if width < RANK:
            inverse_ref[top:below, width:] = jnp.zeros((BLOCK, RANK - width), jnp.float32)
        if below < RANK:
            update = deep_multiply(done[:, : RANK - start].T, done)
            work_ref[below:, start:stop] = work_ref[below:, start:stop] - update[below - start :, :]


def terms(value, count):
    found = []
    for left in range(count - 1, -1, -1):
        term = value.astype(jnp.bfloat16)
        found.append(term)
        if left:
            value = value - term.astype(jnp.float32)
    return found


CHUNKS = 4


def term_multiply(left_terms, right_terms, right_dim=0):
    count = len(right_terms)
    rows = left_terms[0].shape[0]
    total = None
    for order in range(count - 1, -1, -1):
        met = left_terms[: count - order]
        stack = met[0] if len(met) == 1 else jnp.concatenate(met, axis=0)
        product = multiply(stack, right_terms[order], 1, right_dim, None)
        for i in range(len(met) - 1, -1, -1):
            part = product[i * rows : (i + 1) * rows]
            total = part if total is None else total + part
    return total


def pack_gram(rows, quarter, row_lane):
    turned = rows
    for i in range(1, 4):
        turned = jnp.where(quarter == i, pltpu.roll(rows, RANK - 64 * i, 1), turned)
    tiles = [turned[8 * i : 8 * i + 8, :128] for i in range(4)]
    for i in (0, 2):
        first, second = (turned[8 * k : 8 * k + 8, 128:] for k in (i, i + 1))
        tiles.append(jnp.where(row_lane < 64, first, pltpu.roll(second, 64, 1)))
    return tiles


def unpack_gram(tiles, row_lane):
    rows = []
    for i in range(4):
        near = tiles[i] * jnp.where(row_lane < 64, 0.5, 1.0)
        far = tiles[4 + i // 2]
        far = pltpu.roll(far, 64, 1) if i % 2 else far
        rows.append(jnp.concatenate([near, jnp.where(row_lane < 64, 0.5 * far, 0.0)], axis=1))
    return rows


def first_kernel(
    place_ref, gram_ref, left_ref, momentum_ref, gradient_ref,
    once_ref, kept_ref, given_ref, work_ref, inverse_ref, square_ref, right_ref,
    held_momentum, held_gradient, arrived,
):
    quarter, core = place_ref[0], place_ref[1]
    fetches = (
        pltpu.make_async_copy(momentum_ref, held_momentum, arrived.at[0]),
        pltpu.make_async_copy(gradient_ref, held_gradient, arrived.at[1]),
    )
    for fetch in fetches:
        fetch.start()
    invert_factor(gram_ref[...], work_ref, inverse_ref)
    once = multiply(left_ref[...], inverse_ref[...], 1, 1)
    once_ref[...] = once
    turned = terms(once.T, 3)
    square_ref[...] = term_multiply(turned, turned, 1)
    for fetch in fetches:
        fetch.wait()
    buffer = held_momentum[...] + held_gradient[...].astype(jnp.float32)
    right_ref[...] = term_multiply(turned, terms(buffer, 3)).T
    row_lane = lax.broadcasted_iota(jnp.int32, (8, 128), 1)
    size = right_ref.shape[0] // 2
    for target, half in ((kept_ref, core), (given_ref, 1 - core)):
        target[:size, :] = right_ref[pl.ds(pl.multiple_of(half * size, 8), size), :]
        start = pl.multiple_of(quarter * 64 + half * 32, 32)
        tiles = pack_gram(square_ref[pl.ds(start, 32), :], quarter, row_lane)
        for i, tile in enumerate(tiles):
            top, left = size + i // 2 * 8, i % 2 * 128
            target[top : top + 8, left : left + 128] = tile


def second_kernel(place_ref, own_ref, other_ref, once_ref, found_ref, gram_ref, work_ref):
    rows = once_ref.shape[0]
    inverse_ref = found_ref.at[rows:]
    quarter, core = place_ref[0], place_ref[1]
    row_lane = lax.broadcasted_iota(jnp.int32, (8, 128), 1)
    for step in range(4):
        base = lax.rem(quarter + (4 - step), 4) * 64
        for source, half in ((own_ref, core), (other_ref, 1 - core)):
            tiles = [
                source[24 * step + top : 24 * step + top + 8, left : left + 128]
                for top in (0, 8, 16)
                for left in (0, 128)
            ]
            start = pl.multiple_of(base + half * 32, 32)
            for i, part in enumerate(unpack_gram(tiles, row_lane)):
                gram_ref[pl.ds(start + 8 * i, 8), :] = part
    parts = [gram_ref[64 * i : 64 * i + 64, :] for i in range(4)]
    parts = [parts[0]] + [pltpu.roll(parts[i], 64 * i, 1) for i in range(1, 4)]
    gram = jnp.concatenate(parts, axis=0)
    invert_factor(gram + gram.T, work_ref, inverse_ref)
    found_ref[:rows, :] = multiply(once_ref[...], inverse_ref[...], 1, 1)


def third_kernel(part_ref, found_ref, right_ref, square_ref):
    inverse = found_ref[found_ref.shape[0] - RANK :, :]
    right = multiply(part_ref[...], inverse, 1, 1)
    right_ref[...] = right
    squares = jnp.sum(right * right, axis=0, keepdims=True)
    for i in range(square_ref.shape[0]):
        square_ref[i] = squares


def lay_together(core, own_ref, other_ref, whole_ref):
    size = own_ref.shape[0]
    for source, half in ((own_ref, core), (other_ref, 1 - core)):
        whole_ref[pl.ds(pl.multiple_of(half * size, 8), size), :] = source[...]


def fourth_kernel(
    place_ref, momentum_ref, gradient_ref, found_ref, own_ref, other_ref,
    next_ref, held_momentum, held_gradient, right_ref, arrived,
):
    fetches = (
        pltpu.make_async_copy(momentum_ref, held_momentum, arrived.at[0]),
        pltpu.make_async_copy(gradient_ref, held_gradient, arrived.at[1]),
    )
    for fetch in fetches:
        fetch.start()
    lay_together(place_ref[1], own_ref, other_ref, right_ref)
    basis = found_ref[: next_ref.shape[0], :]
    product = term_multiply(terms(basis, 2), terms(right_ref[...], 2), 1)
    for fetch in fetches:
        fetch.wait()
    buffer = held_momentum[...] + held_gradient[...].astype(jnp.float32)
    next_ref[...] = buffer - error_share * product


def fifth_kernel(
    place_ref, squares_ref, found_ref, own_ref, other_ref, next_ref, step_ref,
    next_held, step_held, right_ref, done,
):
    lay_together(place_ref[1], own_ref, other_ref, right_ref)
    square_sum = squares_ref[0]
    for i in range(1, squares_ref.shape[0]):
        square_sum = square_sum + squares_ref[i]
    scale = lax.rsqrt(square_sum * (1.0 / FFW) + 1e-06)
    next_held[...] = right_ref[...] * scale
    writes = [pltpu.make_async_copy(next_held, next_ref, done.at[CHUNKS])]
    writes[0].start()
    rows, width = step_held.shape
    left = terms(found_ref[:rows, :] * (scale * math.sqrt(D / RANK)), 2)
    for i, start in enumerate(range(0, width, RANK)):
        columns = pl.ds(start, min(RANK, width - start))
        step_held[:, columns] = term_multiply(left, terms(right_ref[columns, :], 2), 1)
        writes.append(
            pltpu.make_async_copy(step_held.at[:, columns], step_ref.at[:, columns], done.at[i])
        )
        writes[-1].start()
    for write in writes:
        write.wait()


def sum_kernel(parts_ref, copies_ref, rest_ref=None):
    total = parts_ref[0]
    for i in range(1, parts_ref.shape[0]):
        total = total + parts_ref[i]
    height = copies_ref.shape[1]
    for i in range(copies_ref.shape[0]):
        copies_ref[i] = total[:height]
    if rest_ref is not None:
        rest_ref[...] = total[height:]


def call(kernel, name, operands, outputs, scratch=(), far=(), scalars=True, near=(), out_far=()):
    operands = list(operands)
    in_specs = [pl.BlockSpec(memory_space=pltpu.VMEM)] * len(operands)
    if scalars:
        in_specs[0] = pl.BlockSpec(memory_space=pltpu.SMEM)
    for i in far:
        operands[i] = pltpu.with_memory_space_constraint(operands[i], pltpu.HBM)
        in_specs[i] = pl.BlockSpec(memory_space=pl.ANY)
    out_shape, out_specs = [], []
    for i, output in enumerate(outputs):
        shape, dtype = output if isinstance(output[0], tuple) else (output, jnp.float32)
        out_shape.append(
            pltpu.VMEM(shape, dtype) if i in near else jax.ShapeDtypeStruct(shape, dtype)
        )
        space = pl.ANY if i in out_far else pltpu.VMEM
        out_specs.append(pl.BlockSpec(memory_space=space))
    return pl.pallas_call(
        kernel,
        out_shape=out_shape,
        in_specs=in_specs,
        out_specs=out_specs,
        scratch_shapes=list(scratch),
        compiler_params=pltpu.CompilerParams(vmem_limit_bytes=VMEM),
        cost_estimate=pl.CostEstimate(
            flops=10**9, bytes_accessed=8 * 2**20, transcendentals=0
        ),
        name=name,
    )(*operands)


def room(*shape, dtype=jnp.float32):
    return pltpu.VMEM(shape, dtype)


plane_groups = [
    [(2 * z + core) * TENSOR + t for t in range(TENSOR) for core in range(2)] for z in range(Z)
]
both_axes = ("fsdp", "tensor")


def exchange(block, axis, groups=None):
    return lax.all_to_all(block, axis, 0, 0, axis_index_groups=groups, tiled=True)


def copies(block, members):
    return jnp.broadcast_to(block, (members,) + block.shape)


def swap_cores(block):
    return lax.ppermute(block, "fsdp", [(i, i ^ 1) for i in range(2 * Z)])


def core_half(block, core):
    half = block.shape[0] // 2
    kept = lax.dynamic_slice_in_dim(block, core * half, half)
    given = lax.dynamic_slice_in_dim(block, (1 - core) * half, half)
    return kept + swap_cores(given)


def gram_rows(factor, place):
    width = RANK // TENSOR
    own = lax.dynamic_slice_in_dim(factor, place * width, width, axis=1)
    return multiply(own, factor, 0, 0)


def per_device(momentum, gradient, right_state):
    core = lax.axis_index("fsdp") % 2
    place = lax.axis_index("tensor")
    where = jnp.stack([place % 4, core]).astype(jnp.int32)
    rows, columns = momentum.shape
    held = [room(rows, columns), room(rows, columns, dtype=gradient.dtype)]
    partial_left = multiply(momentum + gradient.astype(jnp.float32), right_state, 1, 0)
    parts = exchange(partial_left.reshape(TENSOR, rows // TENSOR, RANK), "tensor")
    (parts,) = call(sum_kernel, "left_sum", (parts,), (parts.shape,), scalars=False)
    left_raw = exchange(parts, "tensor").reshape(rows, RANK)

    gram_part = core_half(gram_rows(left_raw, place), core)
    parts = exchange(copies(gram_part, Z), "fsdp", z_groups)
    (parts,) = call(
        sum_kernel, "gram_sum", (parts,), ((2 * TENSOR,) + parts.shape[1:],), scalars=False
    )
    gram = exchange(parts, both_axes, plane_groups).reshape(RANK, RANK)
    work = [room(RANK, 2 * RANK), room(RANK, RANK)]
    left_once, kept, given = call(
        first_kernel,
        "first",
        (where, gram, left_raw, momentum, gradient),
        ((rows, RANK), (columns // 2 + 24, RANK), (columns // 2 + 24, RANK)),
        work + [room(RANK, RANK), room(columns, RANK)] + held + [pltpu.SemaphoreType.DMA((2,))],
        far=(3, 4),
        near=(0,),
    )

    part = kept + swap_cores(given)
    size = columns // 2
    parts = jnp.concatenate(
        [part[:size].reshape(Z, size // Z, RANK), copies(part[size:], Z)], axis=1
    )
    parts = exchange(parts, "fsdp", z_groups)
    parts, gram_part = call(
        sum_kernel, "right_sum", (parts,), ((Z, size // Z, RANK), (24, RANK)), scalars=False
    )
    right_part = exchange(parts, "fsdp", z_groups)
    received = [gram_part]
    for step in range(1, 4):
        pairs = [(i, i // 4 * 4 + (i + step) % 4) for i in range(TENSOR)]
        received.append(lax.ppermute(gram_part, "tensor", pairs))
    gram_part = jnp.concatenate(received, axis=0)
    (found,) = call(
        second_kernel,
        "second",
        (where, gram_part, swap_cores(gram_part), left_once),
        ((rows + RANK, RANK),),
        (work[1], work[0]),
        near=(0,),
    )
    right_part, found = lax.optimization_barrier((right_part, found))
    right_part, squares = call(
        third_kernel,
        "third",
        (right_part.reshape(size, RANK), found),
        ((size, RANK), (2 * TENSOR, 1, RANK)),
        scalars=False,
        near=(0,),
    )
    squares = exchange(squares, both_axes, plane_groups)
    other_part = swap_cores(right_part)
    (momentum_next,) = call(
        fourth_kernel,
        "fourth",
        (where, momentum, gradient, found, right_part, other_part),
        ((rows, columns),),
        held + [room(columns, RANK), pltpu.SemaphoreType.DMA((2,))],
        far=(1, 2),
    )
    right_next, step_direction = call(
        fifth_kernel,
        "fifth",
        (where, squares, found, right_part, other_part),
        ((columns, RANK), (rows, columns)),
        [room(columns, RANK), room(rows, columns), room(columns, RANK), pltpu.SemaphoreType.DMA((CHUNKS + 1,))],
        out_far=(0, 1),
    )
    return (momentum_next, right_next, step_direction)


def solution(mesh):
    return jax.shard_map(
        per_device,
        mesh=mesh,
        in_specs=(P("fsdp", "tensor"), P("fsdp", "tensor"), P("tensor", None)),
        out_specs=(P("fsdp", "tensor"), P("tensor", None), P("fsdp", "tensor")),
        check_vma=False,
    )
```

```python
import math

import jax
import jax.numpy as jnp
from jax import lax
from jax.experimental import pallas as pl
from jax.experimental.pallas import tpu as pltpu
from jax.sharding import PartitionSpec as P

D = 8192
FFW = 14336
RANK = 256
BLOCK = 64
VMEM = 20 * 2**20
TENSOR = 16
Z = 8

highest = lax.Precision.HIGHEST
error_share = 0.05
z_groups = [[2 * z + core for z in range(Z)] for core in range(2)]


def multiply(left_side, right_side, left_dim, right_dim, precision=highest):
    return lax.dot_general(
        left_side,
        right_side,
        (((left_dim,), (right_dim,)), ((), ())),
        precision=precision,
        preferred_element_type=jnp.float32,
    )


def spread_lane(tile, lane):
    return jnp.take_along_axis(tile, jnp.full(tile.shape, lane, jnp.int32), axis=1)


def spread_row(tile, row):
    return jnp.broadcast_to(tile[row : row + 1, :], tile.shape)


def factor_block(tiles, first_lane, row_index):
    tiles = list(tiles)
    count = len(tiles)
    own = [spread_lane(tiles[0], first_lane + j) for j in range(8)]
    for s in range(count):
        below = range(s + 1, count)
        columns = [
            {i: spread_lane(tiles[i], first_lane + 8 * s + j) for i in below} for j in range(8)
        ]
        if below:
            following = [
                spread_lane(tiles[s + 1], first_lane + 8 * (s + 1) + j) for j in range(8)
            ]
        steps, own_steps, pivots = [], [], None
        for k in range(8):
            pivot = spread_row(own[k], k)
            inverse_pivot = 1.0 / pivot
            pivots = pivot if pivots is None else jnp.where(row_index == k, pivot, pivots)
            own_step = own[k] * inverse_pivot
            step = {i: columns[k][i] * inverse_pivot for i in below}
            own_steps.append(jnp.where(row_index > k, own_step, 0.0))
            steps.append(step)
            for j in range(k + 1, 8):
                entry = spread_row(own[j], k)
                own[j] = own[j] - own_step * entry
                for i in below:
                    columns[j][i] = columns[j][i] - step[i] * entry
            if below:
                for j in range(8):
                    following[j] = following[j] - step[s + 1] * spread_row(columns[k][s + 1], j)
        tile = tiles[s]
        for k in range(8):
            pivot_row = spread_row(tile, k)
            tile = tile - own_steps[k] * pivot_row
            for i in below:
                tiles[i] = tiles[i] - steps[k][i] * pivot_row
        tiles[s] = tile * lax.rsqrt(pivots)
        own = following
    return tiles


def deep_multiply(left_side, right_side):
    high, middle, low = terms(left_side, 3)
    left = jnp.concatenate([low, high, middle, middle, high, high], axis=1)
    high, middle, low = terms(right_side, 3)
    right = jnp.concatenate([high, low, middle, high, middle, high], axis=0)
    return multiply(left, right, 1, 0, None)


def invert_factor(gram, work_ref, inverse_ref):
    rows = lax.broadcasted_iota(jnp.int32, (RANK, RANK), 0)
    lanes = lax.broadcasted_iota(jnp.int32, (RANK, RANK), 1)
    diagonal = rows == lanes
    ridge = (1e-06 / RANK) * jnp.sum(jnp.where(diagonal, gram, 0.0), keepdims=True)
    work_ref[:, :RANK] = gram + jnp.where(diagonal, ridge, 0.0)
    work_ref[:, RANK:] = jnp.where(diagonal, 1.0, 0.0)
    row_index = lax.broadcasted_iota(jnp.int32, (8, 128), 0)
    lane_index = lax.broadcasted_iota(jnp.int32, (8, 128), 1)
    for block in range(RANK // BLOCK):
        top = block * BLOCK
        aligned = top // 128 * 128
        first_lane = top - aligned
        own_half = lane_index >= 64 if first_lane else lane_index < 64
        tiles = []
        for i in range(BLOCK // 8):
            part = work_ref[top + 8 * i : top + 8 * i + 8, aligned : aligned + 128]
            unit = jnp.where(lane_index == row_index + (8 * i + 64 - first_lane), 1.0, 0.0)
            tiles.append(jnp.where(own_half, part, unit))
        factored = jnp.concatenate(factor_block(tiles, first_lane, row_index), axis=0)
        if first_lane == 0:
            factored = pltpu.roll(factored, 64, 1)
        below = top + BLOCK
        start = RANK if below == RANK else below // 128 * 128
        width = -(-below // 128) * 128
        stop = RANK + width
        done = deep_multiply(factored[:, :BLOCK], work_ref[top:below, start:stop])
        inverse_ref[top:below, :width] = done[:, RANK - start :]
        if width < RANK:
            inverse_ref[top:below, width:] = jnp.zeros((BLOCK, RANK - width), jnp.float32)
        if below < RANK:
            update = deep_multiply(done[:, : RANK - start].T, done)
            work_ref[below:, start:stop] = work_ref[below:, start:stop] - update[below - start :, :]


def terms(value, count):
    found = []
    for left in range(count - 1, -1, -1):
        term = value.astype(jnp.bfloat16)
        found.append(term)
        if left:
            value = value - term.astype(jnp.float32)
    return found


CHUNKS = 4


def term_multiply(left_terms, right_terms, right_dim=0):
    count = len(right_terms)
    rows = left_terms[0].shape[0]
    total = None
    for order in range(count - 1, -1, -1):
        met = left_terms[: count - order]
        stack = met[0] if len(met) == 1 else jnp.concatenate(met, axis=0)
        product = multiply(stack, right_terms[order], 1, right_dim, None)
        for i in range(len(met) - 1, -1, -1):
            part = product[i * rows : (i + 1) * rows]
            total = part if total is None else total + part
    return total


def pack_gram(rows, quarter, row_lane):
    turned = rows
    for i in range(1, 4):
        turned = jnp.where(quarter == i, pltpu.roll(rows, RANK - 64 * i, 1), turned)
    tiles = [turned[8 * i : 8 * i + 8, :128] for i in range(4)]
    for i in (0, 2):
        first, second = (turned[8 * k : 8 * k + 8, 128:] for k in (i, i + 1))
        tiles.append(jnp.where(row_lane < 64, first, pltpu.roll(second, 64, 1)))
    return tiles


def unpack_gram(tiles, row_lane):
    rows = []
    for i in range(4):
        near = tiles[i] * jnp.where(row_lane < 64, 0.5, 1.0)
        far = tiles[4 + i // 2]
        far = pltpu.roll(far, 64, 1) if i % 2 else far
        rows.append(jnp.concatenate([near, jnp.where(row_lane < 64, 0.5 * far, 0.0)], axis=1))
    return rows


def own_place():
    return lax.rem(lax.axis_index("tensor"), 4), lax.rem(lax.axis_index("fsdp"), 2)


def left_kernel(
    momentum_ref, gradient_ref, state_ref, out_ref,
    held_momentum, held_gradient, held_state, arrived,
):
    width = held_momentum.shape[1]
    chunks = []
    for i, start in enumerate(range(0, width, RANK)):
        part = pl.ds(start, min(RANK, width - start))
        fetches = (
            pltpu.make_async_copy(state_ref.at[part], held_state.at[part], arrived.at[3 * i]),
            pltpu.make_async_copy(
                momentum_ref.at[:, part], held_momentum.at[:, part], arrived.at[3 * i + 1]
            ),
            pltpu.make_async_copy(
                gradient_ref.at[:, part], held_gradient.at[:, part], arrived.at[3 * i + 2]
            ),
        )
        for fetch in fetches:
            fetch.start()
        chunks.append((part, fetches))
    total = None
    for part, fetches in chunks:
        for fetch in fetches:
            fetch.wait()
        buffer = held_momentum[:, part] + held_gradient[:, part].astype(jnp.float32)
        product = term_multiply(terms(buffer, 3), terms(held_state[part, :], 3))
        total = product if total is None else total + product
    out_ref[...] = total


def first_kernel(
    gram_ref, left_ref, momentum_ref, gradient_ref,
    once_ref, kept_ref, given_ref, work_ref, inverse_ref, square_ref, right_ref,
    held_momentum, held_gradient, arrived,
):
    quarter, core = own_place()
    fetches = (
        pltpu.make_async_copy(momentum_ref, held_momentum, arrived.at[0]),
        pltpu.make_async_copy(gradient_ref, held_gradient, arrived.at[1]),
    )
    for fetch in fetches:
        fetch.start()
    invert_factor(gram_ref[...], work_ref, inverse_ref)
    once = multiply(left_ref[...], inverse_ref[...], 1, 1)
    once_ref[...] = once
    turned = terms(once.T, 3)
    square_ref[...] = term_multiply(turned, turned, 1)
    for fetch in fetches:
        fetch.wait()
    buffer = held_momentum[...] + held_gradient[...].astype(jnp.float32)
    right_ref[...] = term_multiply(turned, terms(buffer, 3)).T
    row_lane = lax.broadcasted_iota(jnp.int32, (8, 128), 1)
    size = right_ref.shape[0] // 2
    for target, half in ((kept_ref, core), (given_ref, 1 - core)):
        target[:size, :] = right_ref[pl.ds(pl.multiple_of(half * size, 8), size), :]
        start = pl.multiple_of(quarter * 64 + half * 32, 32)
        tiles = pack_gram(square_ref[pl.ds(start, 32), :], quarter, row_lane)
        for i, tile in enumerate(tiles):
            top, left = size + i // 2 * 8, i % 2 * 128
            target[top : top + 8, left : left + 128] = tile


def second_kernel(own_ref, other_ref, once_ref, found_ref, gram_ref, work_ref):
    rows = once_ref.shape[0]
    inverse_ref = found_ref.at[rows:]
    quarter, core = own_place()
    row_lane = lax.broadcasted_iota(jnp.int32, (8, 128), 1)
    for step in range(4):
        base = lax.rem(quarter + (4 - step), 4) * 64
        for source, half in ((own_ref, core), (other_ref, 1 - core)):
            tiles = [
                source[24 * step + top : 24 * step + top + 8, left : left + 128]
                for top in (0, 8, 16)
                for left in (0, 128)
            ]
            start = pl.multiple_of(base + half * 32, 32)
            for i, part in enumerate(unpack_gram(tiles, row_lane)):
                gram_ref[pl.ds(start + 8 * i, 8), :] = part
    parts = [gram_ref[64 * i : 64 * i + 64, :] for i in range(4)]
    parts = [parts[0]] + [pltpu.roll(parts[i], 64 * i, 1) for i in range(1, 4)]
    gram = jnp.concatenate(parts, axis=0)
    invert_factor(gram + gram.T, work_ref, inverse_ref)
    found_ref[:rows, :] = multiply(once_ref[...], inverse_ref[...], 1, 1)


def third_kernel(part_ref, found_ref, right_ref, square_ref):
    inverse = found_ref[found_ref.shape[0] - RANK :, :]
    right = multiply(part_ref[...], inverse, 1, 1)
    right_ref[...] = right
    squares = jnp.sum(right * right, axis=0, keepdims=True)
    for i in range(square_ref.shape[0]):
        square_ref[i] = squares


def lay_together(core, own_ref, other_ref, whole_ref):
    size = own_ref.shape[0]
    for source, half in ((own_ref, core), (other_ref, 1 - core)):
        whole_ref[pl.ds(pl.multiple_of(half * size, 8), size), :] = source[...]


def fourth_kernel(
    momentum_ref, gradient_ref, found_ref, own_ref, other_ref,
    next_ref, held_momentum, held_gradient, right_ref, arrived,
):
    fetches = (
        pltpu.make_async_copy(momentum_ref, held_momentum, arrived.at[0]),
        pltpu.make_async_copy(gradient_ref, held_gradient, arrived.at[1]),
    )
    for fetch in fetches:
        fetch.start()
    lay_together(own_place()[1], own_ref, other_ref, right_ref)
    basis = found_ref[: next_ref.shape[0], :]
    product = term_multiply(terms(basis, 2), terms(right_ref[...], 2), 1)
    for fetch in fetches:
        fetch.wait()
    buffer = held_momentum[...] + held_gradient[...].astype(jnp.float32)
    next_ref[...] = buffer - error_share * product


def fifth_kernel(
    squares_ref, found_ref, own_ref, other_ref, next_ref, step_ref,
    next_held, step_held, right_ref, done,
):
    lay_together(own_place()[1], own_ref, other_ref, right_ref)
    square_sum = squares_ref[0]
    for i in range(1, squares_ref.shape[0]):
        square_sum = square_sum + squares_ref[i]
    scale = lax.rsqrt(square_sum * (1.0 / FFW) + 1e-06)
    next_held[...] = right_ref[...] * scale
    writes = [pltpu.make_async_copy(next_held, next_ref, done.at[CHUNKS])]
    writes[0].start()
    rows, width = step_held.shape
    left = terms(found_ref[:rows, :] * (scale * math.sqrt(D / RANK)), 2)
    for i, start in enumerate(range(0, width, RANK)):
        columns = pl.ds(start, min(RANK, width - start))
        step_held[:, columns] = term_multiply(left, terms(right_ref[columns, :].T, 2))
        writes.append(
            pltpu.make_async_copy(step_held.at[:, columns], step_ref.at[:, columns], done.at[i])
        )
        writes[-1].start()
    for write in writes:
        write.wait()


def sum_kernel(parts_ref, copies_ref, rest_ref=None):
    total = parts_ref[0]
    for i in range(1, parts_ref.shape[0]):
        total = total + parts_ref[i]
    height = copies_ref.shape[1]
    for i in range(copies_ref.shape[0]):
        copies_ref[i] = total[:height]
    if rest_ref is not None:
        rest_ref[...] = total[height:]


def call(kernel, name, operands, outputs, scratch=(), far=(), near=(), out_far=()):
    operands = list(operands)
    in_specs = [pl.BlockSpec(memory_space=pltpu.VMEM)] * len(operands)
    for i in far:
        operands[i] = pltpu.with_memory_space_constraint(operands[i], pltpu.HBM)
        in_specs[i] = pl.BlockSpec(memory_space=pl.ANY)
    out_shape, out_specs = [], []
    for i, output in enumerate(outputs):
        shape, dtype = output if isinstance(output[0], tuple) else (output, jnp.float32)
        out_shape.append(
            pltpu.VMEM(shape, dtype) if i in near else jax.ShapeDtypeStruct(shape, dtype)
        )
        space = pl.ANY if i in out_far else pltpu.VMEM
        out_specs.append(pl.BlockSpec(memory_space=space))
    return pl.pallas_call(
        kernel,
        out_shape=out_shape,
        in_specs=in_specs,
        out_specs=out_specs,
        scratch_shapes=list(scratch),
        compiler_params=pltpu.CompilerParams(vmem_limit_bytes=VMEM),
        cost_estimate=pl.CostEstimate(
            flops=10**9, bytes_accessed=8 * 2**20, transcendentals=0
        ),
        name=name,
    )(*operands)


def room(*shape, dtype=jnp.float32):
    return pltpu.VMEM(shape, dtype)


plane_groups = [
    [(2 * z + core) * TENSOR + t for t in range(TENSOR) for core in range(2)] for z in range(Z)
]
both_axes = ("fsdp", "tensor")


def exchange(block, axis, groups=None):
    return lax.all_to_all(block, axis, 0, 0, axis_index_groups=groups, tiled=True)


def copies(block, members):
    return jnp.broadcast_to(block, (members,) + block.shape)


def swap_cores(block):
    return lax.ppermute(block, "fsdp", [(i, i ^ 1) for i in range(2 * Z)])


def core_half(block, core):
    half = block.shape[0] // 2
    kept = lax.dynamic_slice_in_dim(block, core * half, half)
    given = lax.dynamic_slice_in_dim(block, (1 - core) * half, half)
    return kept + swap_cores(given)


def gram_rows(factor, place):
    width = RANK // TENSOR
    own = lax.dynamic_slice_in_dim(factor, place * width, width, axis=1)
    return multiply(own, factor, 0, 0)


def per_device(momentum, gradient, right_state):
    core = lax.axis_index("fsdp") % 2
    place = lax.axis_index("tensor")
    rows, columns = momentum.shape
    held = [room(rows, columns), room(rows, columns, dtype=gradient.dtype)]
    (partial_left,) = call(
        left_kernel,
        "left",
        (momentum, gradient, right_state),
        ((rows, RANK),),
        held + [room(columns, RANK), pltpu.SemaphoreType.DMA((3 * CHUNKS,))],
        far=(0, 1, 2),
    )
    parts = exchange(partial_left.reshape(TENSOR, rows // TENSOR, RANK), "tensor")
    (parts,) = call(sum_kernel, "left_sum", (parts,), (parts.shape,))
    left_raw = exchange(parts, "tensor").reshape(rows, RANK)

    gram_part = core_half(gram_rows(left_raw, place), core)
    parts = exchange(copies(gram_part, Z), "fsdp", z_groups)
    (parts,) = call(
        sum_kernel, "gram_sum", (parts,), ((2 * TENSOR,) + parts.shape[1:],)
    )
    gram = exchange(parts, both_axes, plane_groups).reshape(RANK, RANK)
    work = [room(RANK, 2 * RANK), room(RANK, RANK)]
    left_once, kept, given = call(
        first_kernel,
        "first",
        (gram, left_raw, momentum, gradient),
        ((rows, RANK), (columns // 2 + 24, RANK), (columns // 2 + 24, RANK)),
        work + [room(RANK, RANK), room(columns, RANK)] + held + [pltpu.SemaphoreType.DMA((2,))],
        far=(2, 3),
        near=(0,),
    )

    part = kept + swap_cores(given)
    size = columns // 2
    parts = jnp.concatenate(
        [part[:size].reshape(Z, size // Z, RANK), copies(part[size:], Z)], axis=1
    )
    parts = exchange(parts, "fsdp", z_groups)
    parts, gram_part = call(
        sum_kernel, "right_sum", (parts,), ((Z, size // Z, RANK), (24, RANK))
    )
    right_part = exchange(parts, "fsdp", z_groups)
    received = [gram_part]
    for step in range(1, 4):
        pairs = [(i, i // 4 * 4 + (i + step) % 4) for i in range(TENSOR)]
        received.append(lax.ppermute(gram_part, "tensor", pairs))
    gram_part = jnp.concatenate(received, axis=0)
    (found,) = call(
        second_kernel,
        "second",
        (gram_part, swap_cores(gram_part), left_once),
        ((rows + RANK, RANK),),
        (work[1], work[0]),
        near=(0,),
    )
    right_part, found = lax.optimization_barrier((right_part, found))
    right_part, squares = call(
        third_kernel,
        "third",
        (right_part.reshape(size, RANK), found),
        ((size, RANK), (2 * TENSOR, 1, RANK)),
        near=(0,),
    )
    squares = exchange(squares, both_axes, plane_groups)
    other_part = swap_cores(right_part)
    (momentum_next,) = call(
        fourth_kernel,
        "fourth",
        (momentum, gradient, found, right_part, other_part),
        ((rows, columns),),
        held + [room(columns, RANK), pltpu.SemaphoreType.DMA((2,))],
        far=(0, 1),
    )
    right_next, step_direction = call(
        fifth_kernel,
        "fifth",
        (squares, found, right_part, other_part),
        ((columns, RANK), (rows, columns)),
        [room(columns, RANK), room(rows, columns), room(columns, RANK), pltpu.SemaphoreType.DMA((CHUNKS + 1,))],
        out_far=(0, 1),
    )
    return (momentum_next, right_next, step_direction)


def solution(mesh):
    return jax.shard_map(
        per_device,
        mesh=mesh,
        in_specs=(P("fsdp", "tensor"), P("fsdp", "tensor"), P("tensor", None)),
        out_specs=(P("fsdp", "tensor"), P("tensor", None), P("fsdp", "tensor")),
        check_vma=False,
    )
```

```python
import math

import jax
import jax.numpy as jnp
from jax import lax
from jax.experimental import pallas as pl
from jax.experimental.pallas import tpu as pltpu
from jax.sharding import PartitionSpec as P

D = 8192
FFW = 14336
RANK = 256
BLOCK = 64
VMEM = 20 * 2**20
TENSOR = 16
Z = 8

highest = lax.Precision.HIGHEST
error_share = 0.05
z_groups = [[2 * z + core for z in range(Z)] for core in range(2)]


def multiply(left_side, right_side, left_dim, right_dim, precision=highest):
    return lax.dot_general(
        left_side,
        right_side,
        (((left_dim,), (right_dim,)), ((), ())),
        precision=precision,
        preferred_element_type=jnp.float32,
    )


def spread_lane(tile, lane):
    return jnp.take_along_axis(tile, jnp.full(tile.shape, lane, jnp.int32), axis=1)


def spread_row(tile, row):
    return jnp.broadcast_to(tile[row : row + 1, :], tile.shape)


def factor_block(tiles, first_lane, row_index):
    tiles = list(tiles)
    count = len(tiles)
    own = [spread_lane(tiles[0], first_lane + j) for j in range(8)]
    for s in range(count):
        below = range(s + 1, count)
        columns = [
            {i: spread_lane(tiles[i], first_lane + 8 * s + j) for i in below} for j in range(8)
        ]
        if below:
            following = [
                spread_lane(tiles[s + 1], first_lane + 8 * (s + 1) + j) for j in range(8)
            ]
        steps, own_steps, pivots = [], [], None
        for k in range(8):
            pivot = spread_row(own[k], k)
            inverse_pivot = 1.0 / pivot
            pivots = pivot if pivots is None else jnp.where(row_index == k, pivot, pivots)
            own_step = own[k] * inverse_pivot
            step = {i: columns[k][i] * inverse_pivot for i in below}
            own_steps.append(jnp.where(row_index > k, own_step, 0.0))
            steps.append(step)
            for j in range(k + 1, 8):
                entry = spread_row(own[j], k)
                own[j] = own[j] - own_step * entry
                for i in below:
                    columns[j][i] = columns[j][i] - step[i] * entry
            if below:
                for j in range(8):
                    following[j] = following[j] - step[s + 1] * spread_row(columns[k][s + 1], j)
        tile = tiles[s]
        for k in range(8):
            pivot_row = spread_row(tile, k)
            tile = tile - own_steps[k] * pivot_row
            for i in below:
                tiles[i] = tiles[i] - steps[k][i] * pivot_row
        tiles[s] = tile * lax.rsqrt(pivots)
        own = following
    return tiles


def deep_multiply(left_side, right_side):
    high, middle, low = terms(left_side, 3)
    left = jnp.concatenate([low, high, middle, middle, high, high], axis=1)
    high, middle, low = terms(right_side, 3)
    right = jnp.concatenate([high, low, middle, high, middle, high], axis=0)
    return multiply(left, right, 1, 0, None)


def invert_factor(gram, work_ref, inverse_ref):
    rows = lax.broadcasted_iota(jnp.int32, (RANK, RANK), 0)
    lanes = lax.broadcasted_iota(jnp.int32, (RANK, RANK), 1)
    diagonal = rows == lanes
    ridge = (1e-06 / RANK) * jnp.sum(jnp.where(diagonal, gram, 0.0), keepdims=True)
    work_ref[:, :RANK] = gram + jnp.where(diagonal, ridge, 0.0)
    work_ref[:, RANK:] = jnp.where(diagonal, 1.0, 0.0)
    row_index = lax.broadcasted_iota(jnp.int32, (8, 128), 0)
    lane_index = lax.broadcasted_iota(jnp.int32, (8, 128), 1)
    for block in range(RANK // BLOCK):
        top = block * BLOCK
        aligned = top // 128 * 128
        first_lane = top - aligned
        own_half = lane_index >= 64 if first_lane else lane_index < 64
        tiles = []
        for i in range(BLOCK // 8):
            part = work_ref[top + 8 * i : top + 8 * i + 8, aligned : aligned + 128]
            unit = jnp.where(lane_index == row_index + (8 * i + 64 - first_lane), 1.0, 0.0)
            tiles.append(jnp.where(own_half, part, unit))
        factored = jnp.concatenate(factor_block(tiles, first_lane, row_index), axis=0)
        if first_lane == 0:
            factored = pltpu.roll(factored, 64, 1)
        below = top + BLOCK
        start = RANK if below == RANK else below // 128 * 128
        width = -(-below // 128) * 128
        stop = RANK + width
        done = deep_multiply(factored[:, :BLOCK], work_ref[top:below, start:stop])
        inverse_ref[top:below, :width] = done[:, RANK - start :]
        if width < RANK:
            inverse_ref[top:below, width:] = jnp.zeros((BLOCK, RANK - width), jnp.float32)
        if below < RANK:
            update = deep_multiply(done[:, : RANK - start].T, done)
            work_ref[below:, start:stop] = work_ref[below:, start:stop] - update[below - start :, :]


def terms(value, count):
    found = []
    for left in range(count - 1, -1, -1):
        term = value.astype(jnp.bfloat16)
        found.append(term)
        if left:
            value = value - term.astype(jnp.float32)
    return found


CHUNKS = 4


def term_multiply(left_terms, right_terms, right_dim=0):
    count = len(right_terms)
    rows = left_terms[0].shape[0]
    total = None
    for order in range(count - 1, -1, -1):
        met = left_terms[: count - order]
        stack = met[0] if len(met) == 1 else jnp.concatenate(met, axis=0)
        product = multiply(stack, right_terms[order], 1, right_dim, None)
        for i in range(len(met) - 1, -1, -1):
            part = product[i * rows : (i + 1) * rows]
            total = part if total is None else total + part
    return total


def pack_gram(rows, quarter, row_lane):
    turned = rows
    for i in range(1, 4):
        turned = jnp.where(quarter == i, pltpu.roll(rows, RANK - 64 * i, 1), turned)
    tiles = [turned[8 * i : 8 * i + 8, :128] for i in range(4)]
    for i in (0, 2):
        first, second = (turned[8 * k : 8 * k + 8, 128:] for k in (i, i + 1))
        tiles.append(jnp.where(row_lane < 64, first, pltpu.roll(second, 64, 1)))
    return tiles


def unpack_gram(tiles, row_lane):
    rows = []
    for i in range(4):
        near = tiles[i] * jnp.where(row_lane < 64, 0.5, 1.0)
        far = tiles[4 + i // 2]
        far = pltpu.roll(far, 64, 1) if i % 2 else far
        rows.append(jnp.concatenate([near, jnp.where(row_lane < 64, 0.5 * far, 0.0)], axis=1))
    return rows


def own_place():
    return lax.rem(lax.axis_index("tensor"), 4), lax.rem(lax.axis_index("fsdp"), 2)


def left_kernel(
    momentum_ref, gradient_ref, state_ref, out_ref,
    held_momentum, held_gradient, held_state, arrived,
):
    width = held_momentum.shape[1]
    chunks = []
    for i, start in enumerate(range(0, width, RANK)):
        part = pl.ds(start, min(RANK, width - start))
        fetches = (
            pltpu.make_async_copy(state_ref.at[part], held_state.at[part], arrived.at[3 * i]),
            pltpu.make_async_copy(
                momentum_ref.at[:, part], held_momentum.at[:, part], arrived.at[3 * i + 1]
            ),
            pltpu.make_async_copy(
                gradient_ref.at[:, part], held_gradient.at[:, part], arrived.at[3 * i + 2]
            ),
        )
        for fetch in fetches:
            fetch.start()
        chunks.append((part, fetches))
    total = None
    for part, fetches in chunks:
        for fetch in fetches:
            fetch.wait()
        buffer = held_momentum[:, part] + held_gradient[:, part].astype(jnp.float32)
        product = term_multiply(terms(buffer, 3), terms(held_state[part, :], 3))
        total = product if total is None else total + product
    out_ref[...] = total


def rows_kernel(left_ref, kept_ref, given_ref, square_ref):
    turned = terms(left_ref[...].T, 3)
    square_ref[...] = term_multiply(turned, turned, 1)
    core = own_place()[1]
    size = kept_ref.shape[0]
    for target, half in ((kept_ref, core), (given_ref, 1 - core)):
        start = (lax.axis_index("tensor") * 2 + half) * size
        target[...] = square_ref[pl.ds(pl.multiple_of(start, size), size), :]


def first_kernel(
    gram_ref, left_ref, momentum_ref, gradient_ref,
    once_ref, kept_ref, given_ref, work_ref, inverse_ref, square_ref, right_ref,
    held_momentum, held_gradient, arrived,
):
    quarter, core = own_place()
    fetches = (
        pltpu.make_async_copy(momentum_ref, held_momentum, arrived.at[0]),
        pltpu.make_async_copy(gradient_ref, held_gradient, arrived.at[1]),
    )
    for fetch in fetches:
        fetch.start()
    invert_factor(gram_ref[...], work_ref, inverse_ref)
    once = multiply(left_ref[...], inverse_ref[...], 1, 1)
    once_ref[...] = once
    turned = terms(once.T, 3)
    square_ref[...] = term_multiply(turned, turned, 1)
    for fetch in fetches:
        fetch.wait()
    buffer = held_momentum[...] + held_gradient[...].astype(jnp.float32)
    right_ref[...] = term_multiply(turned, terms(buffer, 3)).T
    row_lane = lax.broadcasted_iota(jnp.int32, (8, 128), 1)
    size = right_ref.shape[0] // 2
    for target, half in ((kept_ref, core), (given_ref, 1 - core)):
        target[:size, :] = right_ref[pl.ds(pl.multiple_of(half * size, 8), size), :]
        start = pl.multiple_of(quarter * 64 + half * 32, 32)
        tiles = pack_gram(square_ref[pl.ds(start, 32), :], quarter, row_lane)
        for i, tile in enumerate(tiles):
            top, left = size + i // 2 * 8, i % 2 * 128
            target[top : top + 8, left : left + 128] = tile


def second_kernel(own_ref, other_ref, once_ref, found_ref, gram_ref, work_ref):
    rows = once_ref.shape[0]
    inverse_ref = found_ref.at[rows:]
    quarter, core = own_place()
    row_lane = lax.broadcasted_iota(jnp.int32, (8, 128), 1)
    for step in range(4):
        base = lax.rem(quarter + (4 - step), 4) * 64
        for source, half in ((own_ref, core), (other_ref, 1 - core)):
            tiles = [
                source[24 * step + top : 24 * step + top + 8, left : left + 128]
                for top in (0, 8, 16)
                for left in (0, 128)
            ]
            start = pl.multiple_of(base + half * 32, 32)
            for i, part in enumerate(unpack_gram(tiles, row_lane)):
                gram_ref[pl.ds(start + 8 * i, 8), :] = part
    parts = [gram_ref[64 * i : 64 * i + 64, :] for i in range(4)]
    parts = [parts[0]] + [pltpu.roll(parts[i], 64 * i, 1) for i in range(1, 4)]
    gram = jnp.concatenate(parts, axis=0)
    invert_factor(gram + gram.T, work_ref, inverse_ref)
    found_ref[:rows, :] = multiply(once_ref[...], inverse_ref[...], 1, 1)


def third_kernel(part_ref, found_ref, right_ref, square_ref):
    inverse = found_ref[found_ref.shape[0] - RANK :, :]
    right = multiply(part_ref[...], inverse, 1, 1)
    right_ref[...] = right
    squares = jnp.sum(right * right, axis=0, keepdims=True)
    for i in range(square_ref.shape[0]):
        square_ref[i] = squares


def lay_together(core, own_ref, other_ref, whole_ref):
    size = own_ref.shape[0]
    for source, half in ((own_ref, core), (other_ref, 1 - core)):
        whole_ref[pl.ds(pl.multiple_of(half * size, 8), size), :] = source[...]


def fourth_kernel(
    momentum_ref, gradient_ref, found_ref, own_ref, other_ref,
    next_ref, held_momentum, held_gradient, right_ref, arrived,
):
    fetches = (
        pltpu.make_async_copy(momentum_ref, held_momentum, arrived.at[0]),
        pltpu.make_async_copy(gradient_ref, held_gradient, arrived.at[1]),
    )
    for fetch in fetches:
        fetch.start()
    lay_together(own_place()[1], own_ref, other_ref, right_ref)
    basis = found_ref[: next_ref.shape[0], :]
    product = term_multiply(terms(basis, 2), terms(right_ref[...], 2), 1)
    for fetch in fetches:
        fetch.wait()
    buffer = held_momentum[...] + held_gradient[...].astype(jnp.float32)
    next_ref[...] = buffer - error_share * product


def fifth_kernel(
    squares_ref, found_ref, own_ref, other_ref, next_ref, step_ref,
    next_held, step_held, right_ref, done,
):
    lay_together(own_place()[1], own_ref, other_ref, right_ref)
    square_sum = squares_ref[0]
    for i in range(1, squares_ref.shape[0]):
        square_sum = square_sum + squares_ref[i]
    scale = lax.rsqrt(square_sum * (1.0 / FFW) + 1e-06)
    next_held[...] = right_ref[...] * scale
    writes = [pltpu.make_async_copy(next_held, next_ref, done.at[CHUNKS])]
    writes[0].start()
    rows, width = step_held.shape
    left = terms(found_ref[:rows, :] * (scale * math.sqrt(D / RANK)), 2)
    for i, start in enumerate(range(0, width, RANK)):
        columns = pl.ds(start, min(RANK, width - start))
        step_held[:, columns] = term_multiply(left, terms(right_ref[columns, :].T, 2))
        writes.append(
            pltpu.make_async_copy(step_held.at[:, columns], step_ref.at[:, columns], done.at[i])
        )
        writes[-1].start()
    for write in writes:
        write.wait()


def sum_kernel(parts_ref, copies_ref, rest_ref=None):
    total = parts_ref[0]
    for i in range(1, parts_ref.shape[0]):
        total = total + parts_ref[i]
    height = copies_ref.shape[1]
    for i in range(copies_ref.shape[0]):
        copies_ref[i] = total[:height]
    if rest_ref is not None:
        rest_ref[...] = total[height:]


def call(kernel, name, operands, outputs, scratch=(), far=(), near=(), out_far=()):
    operands = list(operands)
    in_specs = [pl.BlockSpec(memory_space=pltpu.VMEM)] * len(operands)
    for i in far:
        operands[i] = pltpu.with_memory_space_constraint(operands[i], pltpu.HBM)
        in_specs[i] = pl.BlockSpec(memory_space=pl.ANY)
    out_shape, out_specs = [], []
    for i, output in enumerate(outputs):
        shape, dtype = output if isinstance(output[0], tuple) else (output, jnp.float32)
        out_shape.append(
            pltpu.VMEM(shape, dtype) if i in near else jax.ShapeDtypeStruct(shape, dtype)
        )
        space = pl.ANY if i in out_far else pltpu.VMEM
        out_specs.append(pl.BlockSpec(memory_space=space))
    return pl.pallas_call(
        kernel,
        out_shape=out_shape,
        in_specs=in_specs,
        out_specs=out_specs,
        scratch_shapes=list(scratch),
        compiler_params=pltpu.CompilerParams(vmem_limit_bytes=VMEM),
        cost_estimate=pl.CostEstimate(
            flops=10**9, bytes_accessed=8 * 2**20, transcendentals=0
        ),
        name=name,
    )(*operands)


def room(*shape, dtype=jnp.float32):
    return pltpu.VMEM(shape, dtype)


plane_groups = [
    [(2 * z + core) * TENSOR + t for t in range(TENSOR) for core in range(2)] for z in range(Z)
]
both_axes = ("fsdp", "tensor")


def exchange(block, axis, groups=None):
    return lax.all_to_all(block, axis, 0, 0, axis_index_groups=groups, tiled=True)


def copies(block, members):
    return jnp.broadcast_to(block, (members,) + block.shape)


def swap_cores(block):
    return lax.ppermute(block, "fsdp", [(i, i ^ 1) for i in range(2 * Z)])


def per_device(momentum, gradient, right_state):
    rows, columns = momentum.shape
    held = [room(rows, columns), room(rows, columns, dtype=gradient.dtype)]
    (partial_left,) = call(
        left_kernel,
        "left",
        (momentum, gradient, right_state),
        ((rows, RANK),),
        held + [room(columns, RANK), pltpu.SemaphoreType.DMA((3 * CHUNKS,))],
        far=(0, 1, 2),
    )
    parts = exchange(partial_left.reshape(TENSOR, rows // TENSOR, RANK), "tensor")
    (parts,) = call(sum_kernel, "left_sum", (parts,), (parts.shape,))
    left_raw = exchange(parts, "tensor").reshape(rows, RANK)

    share = (RANK // (2 * TENSOR), RANK)
    kept, given = call(rows_kernel, "rows", (left_raw,), (share, share), [room(RANK, RANK)])
    gram_part = kept + swap_cores(given)
    parts = exchange(copies(gram_part, Z), "fsdp", z_groups)
    (parts,) = call(
        sum_kernel, "gram_sum", (parts,), ((2 * TENSOR,) + parts.shape[1:],)
    )
    gram = exchange(parts, both_axes, plane_groups).reshape(RANK, RANK)
    work = [room(RANK, 2 * RANK), room(RANK, RANK)]
    left_once, kept, given = call(
        first_kernel,
        "first",
        (gram, left_raw, momentum, gradient),
        ((rows, RANK), (columns // 2 + 24, RANK), (columns // 2 + 24, RANK)),
        work + [room(RANK, RANK), room(columns, RANK)] + held + [pltpu.SemaphoreType.DMA((2,))],
        far=(2, 3),
        near=(0,),
    )

    part = kept + swap_cores(given)
    size = columns // 2
    parts = jnp.concatenate(
        [part[:size].reshape(Z, size // Z, RANK), copies(part[size:], Z)], axis=1
    )
    parts = exchange(parts, "fsdp", z_groups)
    parts, gram_part = call(
        sum_kernel, "right_sum", (parts,), ((Z, size // Z, RANK), (24, RANK))
    )
    right_part = exchange(parts, "fsdp", z_groups)
    received = [gram_part]
    for step in range(1, 4):
        pairs = [(i, i // 4 * 4 + (i + step) % 4) for i in range(TENSOR)]
        received.append(lax.ppermute(gram_part, "tensor", pairs))
    gram_part = jnp.concatenate(received, axis=0)
    (found,) = call(
        second_kernel,
        "second",
        (gram_part, swap_cores(gram_part), left_once),
        ((rows + RANK, RANK),),
        (work[1], work[0]),
        near=(0,),
    )
    right_part, found = lax.optimization_barrier((right_part, found))
    right_part, squares = call(
        third_kernel,
        "third",
        (right_part.reshape(size, RANK), found),
        ((size, RANK), (2 * TENSOR, 1, RANK)),
        near=(0,),
    )
    squares = exchange(squares, both_axes, plane_groups)
    other_part = swap_cores(right_part)
    (momentum_next,) = call(
        fourth_kernel,
        "fourth",
        (momentum, gradient, found, right_part, other_part),
        ((rows, columns),),
        held + [room(columns, RANK), pltpu.SemaphoreType.DMA((2,))],
        far=(0, 1),
    )
    right_next, step_direction = call(
        fifth_kernel,
        "fifth",
        (squares, found, right_part, other_part),
        ((columns, RANK), (rows, columns)),
        [room(columns, RANK), room(rows, columns), room(columns, RANK), pltpu.SemaphoreType.DMA((CHUNKS + 1,))],
        out_far=(0, 1),
    )
    return (momentum_next, right_next, step_direction)


def solution(mesh):
    return jax.shard_map(
        per_device,
        mesh=mesh,
        in_specs=(P("fsdp", "tensor"), P("fsdp", "tensor"), P("tensor", None)),
        out_specs=(P("fsdp", "tensor"), P("tensor", None), P("fsdp", "tensor")),
        check_vma=False,
    )
```
